128 devices in a mesh: grp: 16 (over x, z), sub: 8 (over y, core).
Axes of the slice: x: 4, y: 4, z: 4, core: 2. Of those that a mesh axis runs over, the one named last changes fastest.
Arguments:
- embed: float32 [98304, 1024], P(('grp', 'sub'))
- cluster: int32 [98304], P(('grp', 'sub')), may hold values from 0 to 1023, as said below
- rank: int32 [98304], P(('grp', 'sub')), may hold values from 0 to 767, as said below
- target: int32 [98304], P(('grp', 'sub')), may hold values from 0 to 98303, as said below
Outputs:
- best: float32 [98304], P(('grp', 'sub'))
The draws below stay inside these ranges and needn't reach their ends.
Inputs may be any that keep to these rules, and one draw needn't show every extreme that they name: `target`: A permutation: document i goes to row target_i mod 768 of device target_i divided by 768, rounded down, the devices numbered over grp+sub. All documents of one cluster go to devices of one grp index. One device's shard sends at most 12 documents to any one device, and exactly 12 to some. Within a grp index, the row of a document in the group's order (its device's sub index times 768 plus its row) is the number of the group's documents in lower-numbered clusters plus its rank. `cluster`: clusters of one grp index are numbered from that index times 64. `rank`: the ranks inside one cluster are distinct and run from 0 to its size minus 1; the largest cluster of each grp index has 768 documents.
All inputs are finite; a program needn't handle non-finite values.
Results may differ from the reference program's by a relative error of at most 0.00037.
Values may be sent and summed in bfloat16 or wider, within the bound.
A program may use at most 64 MiB of HBM per device.

```python
import math
import jax
import jax.numpy as jnp
from jax import lax

D = 1024
ROWS = 768
ROOT = 8
DOCS = 98304
LARGEST = 768
HOPS = 1
N_GRP = 16
N_SUB = 8


def layout(key):
    devices = N_GRP * N_SUB
    group_rows = ROWS * N_SUB
    clusters_here = ROOT * ROOT
    mean_count = ROWS // devices
    keys = jax.random.split(jax.random.fold_in(key, 101), 7)
    spread = jax.random.randint(keys[0], (devices // 2,), -(mean_count - 1), mean_count)
    spread = spread.at[0].set(mean_count)
    paired = jnp.stack([mean_count + spread, mean_count - spread], axis=1).reshape(devices)
    circle = jax.random.permutation(keys[1], paired)
    owner_perm = jax.random.permutation(keys[2], devices)
    sources = jnp.arange(devices)
    counts = circle[(owner_perm[None, :] - sources[:, None]) % devices]
    col_first = jnp.cumsum(counts, axis=0) - counts
    row_first = jnp.cumsum(counts, axis=1) - counts

    def one_source(source, counts_row, col_row, row_row):
        owner_seq = jnp.repeat(jnp.arange(devices), counts_row, total_repeat_length=ROWS)
        within = jnp.arange(ROWS) - row_row[owner_seq]
        placed = owner_seq * ROWS + col_row[owner_seq] + within
        order = jax.random.permutation(jax.random.fold_in(keys[3], source), ROWS)
        return placed[order]
    placed_all = jax.vmap(one_source)(sources, counts, col_first, row_first).reshape(-1)

    def block_shuffle(device):
        return jax.random.permutation(jax.random.fold_in(keys[6], device), ROWS)
    shuffles = jax.vmap(block_shuffle)(sources)
    owner_of = placed_all // ROWS
    target = owner_of * ROWS + shuffles[owner_of, placed_all % ROWS]
    rest = group_rows - LARGEST
    weights = jax.random.randint(keys[4], (N_GRP, clusters_here - 1), 1, 4)
    cum_w = jnp.cumsum(weights, axis=1)
    total_w = cum_w[:, -1:]
    bounds = rest * cum_w // total_w
    others = bounds - jnp.concatenate([jnp.zeros((N_GRP, 1), bounds.dtype), bounds[:, :-1]], axis=1)
    largest_at = jax.random.randint(keys[5], (N_GRP, 1), 0, clusters_here)
    slots = jnp.arange(clusters_here)[None, :]
    same_pick = jnp.take_along_axis(others, jnp.broadcast_to(jnp.minimum(slots, clusters_here - 2), (N_GRP, clusters_here)), axis=1)
    prev_pick = jnp.take_along_axis(others, jnp.broadcast_to(jnp.maximum(slots - 1, 0), (N_GRP, clusters_here)), axis=1)
    sizes = jnp.where(slots < largest_at, same_pick, jnp.where(slots == largest_at, LARGEST, prev_pick))
    starts = jnp.cumsum(sizes, axis=1) - sizes
    position = jnp.arange(N_GRP * group_rows)
    group_of = position // group_rows
    in_group = position % group_rows
    row_starts = starts[group_of]
    local_cluster = jnp.sum((row_starts <= in_group[:, None]).astype(jnp.int32), axis=1) - 1
    cluster_start = jnp.sum(jnp.where(slots == local_cluster[:, None], row_starts, 0), axis=1)
    owner_cluster = group_of * clusters_here + local_cluster
    owner_rank = in_group - cluster_start
    return (target.astype(jnp.int32), owner_cluster[target].astype(jnp.int32), owner_rank[target].astype(jnp.int32))


def draw_target(key, part):
    target, cluster, rank = layout(key)
    return target


def draw_cluster(key, part):
    target, cluster, rank = layout(key)
    return cluster


def draw_rank(key, part):
    target, cluster, rank = layout(key)
    return rank


def draw_embed(key, part):
    target, cluster, rank = layout(key)
    key = jax.random.fold_in(key, 7)
    keys = jax.random.split(key, 3)
    centers = jax.random.normal(keys[0], (N_GRP * ROOT * ROOT, D), jnp.float32)
    noise = jax.random.normal(keys[1], (DOCS, D), jnp.float32)
    scales = jnp.exp(jax.random.uniform(keys[2], (DOCS, 1), jnp.float32, minval=0.0, maxval=math.log(10.0)))
    return (scales * (0.7 * centers[cluster] + noise)).astype(jnp.float32)


def setup_inputs(seed: int = 0) -> dict:
    streams_of = jax.random.split(jax.random.key(seed), 5)
    embed = draw_embed(jax.random.fold_in(streams_of[4], 71), 0)
    cluster = draw_cluster(jax.random.fold_in(streams_of[4], 71), 0)
    rank = draw_rank(jax.random.fold_in(streams_of[4], 71), 0)
    target = draw_target(jax.random.fold_in(streams_of[4], 71), 0)
    return {"embed": embed, "cluster": cluster, "rank": rank, "target": target}


def reference(embed, cluster, rank, target):
    squares = lax.optimization_barrier(jnp.sum(embed * embed, axis=1, keepdims=True))
    unit_rows = (embed * lax.rsqrt(squares + 1e-06)).astype(jnp.bfloat16)
    owned = jnp.zeros_like(unit_rows).at[target].set(unit_rows)
    own_cluster = jnp.zeros((DOCS,), jnp.int32).at[target].set(cluster)
    own_rank = jnp.zeros((DOCS,), jnp.int32).at[target].set(rank)
    group_rows = ROWS * N_SUB
    window = (HOPS + 1) * ROWS
    group_units = owned.reshape(N_GRP, group_rows, D)
    group_clusters = own_cluster.reshape(N_GRP, group_rows)
    group_ranks = own_rank.reshape(N_GRP, group_rows)

    def per_group(inputs):
        units, clusters, ranks = inputs

        def per_block(block_index):
            first = (block_index * ROWS).astype(jnp.int32)
            left = lax.dynamic_slice_in_dim(units, first, ROWS, 0)
            left_cluster = lax.dynamic_slice_in_dim(clusters, first, ROWS, 0)
            left_rank = lax.dynamic_slice_in_dim(ranks, first, ROWS, 0)
            start = (jnp.maximum(block_index - HOPS, 0) * ROWS).astype(jnp.int32)
            cols = lax.dynamic_slice_in_dim(units, start, window, 0)
            col_cluster = lax.dynamic_slice_in_dim(clusters, start, window, 0)
            col_rank = lax.dynamic_slice_in_dim(ranks, start, window, 0)
            scores = lax.dot_general(left, cols, (((1,), (1,)), ((), ())), preferred_element_type=jnp.float32)
            allowed = (left_cluster[:, None] == col_cluster[None, :]) & (col_rank[None, :] < left_rank[:, None])
            return lax.optimization_barrier(jnp.max(jnp.where(allowed, scores, -1.0), axis=1))
        return lax.map(per_block, jnp.arange(N_SUB, dtype=jnp.int32)).reshape(group_rows)
    best_rows = lax.map(per_group, (group_units, group_clusters, group_ranks))
    return best_rows.reshape(DOCS)
```

```python
import functools

import jax
import jax.numpy as jnp
from jax import lax
from jax.experimental import pallas as pl
from jax.experimental.pallas import tpu as pltpu
from jax.sharding import PartitionSpec as P

MESH = pl.DeviceIdType.MESH
AXES = ("x", "z", "y", "c")
SIZE = {"x": 4, "z": 4, "y": 4, "c": 2}
ORDERS = (("x", "y", "z"), ("y", "z", "x"), ("z", "x", "y"))
ROWS = 768
WIDTH = 1024
HALF = 512
CAP = 12
GROUPS = 3
DEPTH = 4
DEVICES = 128
EDGE = 384
NT = (((1,), (1,)), ((), ()))
bf16, f32, i32 = jnp.bfloat16, jnp.float32, jnp.int32


def view(ref, *lead, **fixed):
    return ref.at[tuple(lead) + tuple(fixed.get(a, slice(None)) for a in AXES)]


def iota(shape, dim):
    return lax.broadcasted_iota(i32, shape, dim)


def dot(a, b, dims=(((1,), (0,)), ((), ())), exact=False):
    precision = lax.Precision.HIGHEST if exact else None
    return lax.dot_general(a, b, dims, precision=precision, preferred_element_type=f32)


def kernel(
    embed_hbm, target_ref, rank_ref, best_ref,
    embed, unit, sent0, sent1, sent2, sent3, meta0, meta1, meta2, meta3, flat,
    slots, chosen, own, from_prev, from_next, returned, answer,
    load_sem, sem1, sem2, sem3, out_sem, msem1, msem2, msem3, mout_sem,
    halo_sem, halo_out, back_sem, back_out,
):
    grp, sub = lax.axis_index("grp"), lax.axis_index("sub")
    me = {"x": grp // 4, "z": lax.rem(grp, 4), "y": sub // 2, "c": lax.rem(sub, 2)}

    def device(**other):
        at = {**me, **other}
        return (at["x"] * 4 + at["z"], at["y"] * 2 + at["c"])

    def around(axis, by):
        return lax.rem(me[axis] + by, 4)

    def remote(src, dst, send_sem, recv_sem, to):
        pltpu.make_async_remote_copy(
            src_ref=src, dst_ref=dst, send_sem=send_sem, recv_sem=recv_sem,
            device_id=to, device_id_type=MESH,
        ).start()

    def landed(ref, sem):
        pltpu.make_async_copy(ref, ref, sem).wait()

    loads = []
    for i in range(3):
        part = pl.ds(i * 256, 256)
        loads.append(pltpu.make_async_copy(embed_hbm.at[part], embed.at[part], load_sem.at[i]))
        loads[-1].start()

    barrier = pltpu.get_barrier_semaphore()
    partners = [device(**{a: around(a, d)}) for a in "xyz" for d in (1, 2, 3)]
    partners += [device(**{a: around(a, d), "c": 1 - me["c"]}) for a in "xyz" for d in (1, 2, 3)]
    partners += [device(c=1 - me["c"])]
    for to in partners:
        pl.semaphore_signal(barrier, inc=1, device_id=to, device_id_type=MESH)

    target = target_ref[...].astype(f32)
    rank = rank_ref[...].astype(f32)
    owner = jnp.floor((target + 0.5) * (1.0 / ROWS))
    row = target - owner * ROWS
    owns = (owner == iota((DEVICES, ROWS), 0).astype(f32)).astype(f32)
    before = (iota((ROWS, ROWS), 0) < iota((ROWS, ROWS), 1)).astype(f32).astype(bf16)
    count = dot(owns.astype(bf16), before)
    within = jnp.sum(owns * count, axis=0, keepdims=True)
    code = owner * CAP + within
    lane_slot = iota((DEVICES, ROWS), 0).astype(f32)
    spread = jnp.where(within == lane_slot, row + 1.0, 0.0) + jnp.where(
        within + 16.0 == lane_slot, rank, 0.0
    )
    flat[...] = dot(owns, spread, NT, exact=True)
    for x in range(4):
        for z in range(4):
            for y in range(4):
                for c in range(2):
                    at = ((x * 4 + z) * 4 + y) * 2 + c
                    meta0[x, z, y, c] = flat[at : at + 1, :]

    for i in range(3):
        loads[i].wait()

        def normalise(j, _):
            part = pl.ds(pl.multiple_of(i * 256 + j * 64, 64), 64)
            e = embed[part, :]
            squares = jnp.sum(e * e, axis=1, keepdims=True)
            unit[part, :] = (e * lax.rsqrt(squares + 1e-06)).astype(bf16)
            return 0

        lax.fori_loop(0, 4, normalise, 0)

    pl.semaphore_wait(barrier, len(partners))

    def meta_first():
        for d in (1, 3, 2):
            t = around("x", d)
            remote(view(meta0, x=t), view(meta1, x=me["x"]), mout_sem.at[0], msem1, device(x=t))
        pltpu.make_async_copy(view(meta0, x=me["x"]), view(meta1, x=me["x"]), msem1).start()

    def meta_second():
        landed(meta1, msem1)
        for d in (1, 3, 2):
            t = around("z", d)
            remote(view(meta1, z=t), view(meta2, z=me["z"]), mout_sem.at[1], msem2, device(z=t))
        pltpu.make_async_copy(view(meta1, z=me["z"]), view(meta2, z=me["z"]), msem2).start()

    def meta_third():
        landed(meta2, msem2)
        for d in (1, 3, 2, 0):
            t = around("y", d)
            for c in (me["c"], 1 - me["c"]):
                if d == 0 and c is me["c"]:
                    continue
                remote(
                    view(meta2, y=t, c=c), view(meta3, y=me["y"], c=me["c"]),
                    mout_sem.at[2], msem3, device(y=t, c=c),
                )
        here = {"y": me["y"], "c": me["c"]}
        pltpu.make_async_copy(view(meta2, **here), view(meta3, **here), msem3).start()

    def pack(h, g):
        k = iota((DEVICES * DEPTH, ROWS), 0)
        wanted = 3 * k - 2 * (k & 3) + DEPTH * g
        pick = (code.astype(i32) == wanted).astype(f32).astype(bf16)
        q = dot(pick, unit[:, h * HALF : (h + 1) * HALF]).reshape(64, 8, HALF)
        r = pltpu.roll(q, 4, 1)
        low = iota((64, 8, 128), 1) < 4
        qs = [q[:, :, 128 * j : 128 * j + 128] for j in range(4)]
        rs = [r[:, :, 128 * j : 128 * j + 128] for j in range(4)]
        even = jnp.concatenate([jnp.where(low, qs[0], rs[1]), jnp.where(low, qs[2], rs[3])], axis=1)
        odd = jnp.concatenate([jnp.where(low, rs[0], qs[1]), jnp.where(low, rs[2], qs[3])], axis=1)
        sent0[h, g, :, :, :, 0] = even.astype(bf16).reshape(4, 4, 4, 16, 128)
        sent0[h, g, :, :, :, 1] = odd.astype(bf16).reshape(4, 4, 4, 16, 128)

    def first(h, g):
        a = ORDERS[g][0]
        for d in (1, 3, 2):
            t = around(a, d)
            remote(
                view(sent0, h, g, **{a: t}), view(sent1, h, g, **{a: me[a]}),
                out_sem.at[h, g, 0], sem1.at[h, g, me[a]], device(**{a: t}),
            )
        here = {a: me[a]}
        pltpu.make_async_copy(
            view(sent0, h, g, **here), view(sent1, h, g, **here), sem1.at[h, g, me[a]]
        ).start()

    def second(h, g, d0):
        a, b, _ = ORDERS[g]
        s = around(a, d0)
        landed(view(sent1, h, g, **{a: s}), sem1.at[h, g, s])
        for d in (1, 3, 2):
            t = around(b, d)
            remote(
                view(sent1, h, g, **{a: s, b: t}), view(sent2, h, g, **{a: s, b: me[b]}),
                out_sem.at[h, g, 1], sem2.at[h, g, me[b]], device(**{b: t}),
            )
        here = {a: s, b: me[b]}
        pltpu.make_async_copy(
            view(sent1, h, g, **here), view(sent2, h, g, **here), sem2.at[h, g, me[b]]
        ).start()

    def third(h, g, d0):
        _, b, e = ORDERS[g]
        s = around(b, d0)
        landed(view(sent2, h, g, **{b: s}), sem2.at[h, g, s])
        for d in (1, 3, 2, 0):
            t = around(e, d)
            for c in (me["c"], 1 - me["c"]):
                if d == 0 and c is me["c"]:
                    continue
                remote(
                    view(sent2, h, g, **{b: s, e: t, "c": c}),
                    view(sent3, h, g, **{b: s, e: me[e], "c": me["c"]}),
                    out_sem.at[h, g, 2], sem3.at[h, g], device(**{e: t, "c": c}),
                )
        here = {b: s, e: me[e], "c": me["c"]}
        pltpu.make_async_copy(
            view(sent2, h, g, **here), view(sent3, h, g, **here), sem3.at[h, g]
        ).start()

    def unpack(h, g):
        landed(sent3.at[h, g], sem3.at[h, g])
        even = sent3[h, g, :, :, :, 0].reshape(64, 16, 128).astype(f32)
        odd = sent3[h, g, :, :, :, 1].reshape(64, 16, 128).astype(f32)
        low = iota((64, 8, 128), 1) < 4
        for j in range(2):
            a, b = even[:, 8 * j : 8 * j + 8], odd[:, 8 * j : 8 * j + 8]
            p = jnp.where(low, a, pltpu.roll(b, 4, 1)).reshape(512, 128)
            q = jnp.where(low, pltpu.roll(a, 4, 1), b).reshape(512, 128)
            slots[g * 512 : g * 512 + 512, 256 * j : 256 * j + 128] = p.astype(bf16)
            slots[g * 512 : g * 512 + 512, 256 * j + 128 : 256 * j + 256] = q.astype(bf16)

    def gather(h):
        def rows(j, _):
            part = pl.ds(pl.multiple_of(j * 256, 256), 256)
            own[h, part, :] = dot(chosen[part, :], slots[...]).astype(bf16)
            return 0

        lax.fori_loop(0, 3, rows, 0)

    later = (grp, lax.rem(sub + 1, 8))
    sooner = (grp, lax.rem(sub + 7, 8))

    def halo(h):
        remote(
            own.at[h, pl.ds(ROWS - EDGE, EDGE)], from_prev.at[h],
            halo_out.at[h, 0], halo_sem.at[h, 0], later,
        )
        remote(
            own.at[h, pl.ds(0, EDGE)], from_next.at[h],
            halo_out.at[h, 1], halo_sem.at[h, 1], sooner,
        )

    def choose():
        landed(meta3, msem3)
        for x in range(4):
            for z in range(4):
                for y in range(4):
                    for c in range(2):
                        at = ((x * 4 + z) * 4 + y) * 2 + c
                        flat[at : at + 1, :] = meta3[x, z, y, c]
        got = flat[...]
        l, k = iota((128, 768), 0), iota((128, 768), 1)
        g, kind = (k // 128) % 3, k // 384
        expand = (l == kind * 16 + g * DEPTH + (k & 3)).astype(f32)
        wide = dot(got, expand, exact=True)
        mine = (iota((32, 128), 1) >> 2) == iota((32, 128), 0)

        def lanes(first):
            pieces = []
            for g in range(GROUPS):
                for j in range(4):
                    v = wide[32 * j : 32 * j + 32, first + 128 * g : first + 128 * g + 128]
                    pieces.append(jnp.sum(jnp.where(mine, v, 0.0), axis=0, keepdims=True))
            return jnp.concatenate(pieces, axis=1)

        place, its_rank = lanes(0), lanes(384)

        def build(j, _):
            part = pl.ds(pl.multiple_of(j * 64, 64), 64)
            r = (iota((64, 1536), 0) + j * 64 + 1).astype(f32)
            chosen[part, :] = (place == r).astype(f32).astype(bf16)
            return 0

        lax.fori_loop(0, 12, build, 0)
        high = jnp.floor(its_rank * (1.0 / 256.0))
        which = iota((16, 1536), 0)
        both = jnp.where(which == 0, high, jnp.where(which == 1, its_rank - 256.0 * high, 0.0))
        ranks = dot(both.astype(bf16), chosen[...], NT)
        rank_of = ranks[0:1] * 256.0 + ranks[1:2]
        return iota((1, ROWS), 1) - rank_of.astype(i32), rank_of[:, ROWS - 1 : ROWS].astype(i32)

    meta_first()
    for g in range(GROUPS):
        pack(0, g)
        first(0, g)
    for g in range(GROUPS):
        second(0, g, 0)
    meta_second()
    for g in range(GROUPS):
        pack(1, g)
    for d in (1, 3, 2):
        for g in range(GROUPS):
            second(0, g, d)
    for g in range(GROUPS):
        first(1, g)
    meta_third()
    for d in (0, 1, 3, 2):
        for g in range(GROUPS):
            third(0, g, d)
    for d in (0, 1, 3, 2):
        for g in range(GROUPS):
            second(1, g, d)
    begin, last_rank = choose()
    for g in range(GROUPS):
        unpack(0, g)
    gather(0)
    halo(0)
    for d in (0, 1, 3, 2):
        for g in range(GROUPS):
            third(1, g, d)
    for g in range(GROUPS):
        unpack(1, g)
    gather(1)
    halo(1)

    def scores(left, right):
        return dot(left[0], right[0], NT) + dot(left[1], right[1], NT)

    here = []
    for j in range(3):
        n = 256 * (j + 1)
        p = slice(256 * j, n)
        s = scores((own[0, 0:n], own[1, 0:n]), (own[0, p], own[1, p]))
        q, at = iota((n, 256), 0), iota((n, 256), 1) + 256 * j
        s = jnp.where((q >= begin[:, p]) & (q < at), s, -1.0)
        here.append(jnp.max(s, axis=0, keepdims=True))
    best = jnp.concatenate(here, axis=1)

    for h in range(2):
        landed(from_next.at[h], halo_sem.at[h, 1])
    s = scores((own[0], own[1]), (from_next[0], from_next[1]))
    s = jnp.where(iota((ROWS, EDGE), 0) >= ROWS - 1 - last_rank, s, -1.0)
    answer[...] = jnp.max(s, axis=0, keepdims=True)
    remote(answer, returned, back_out, back_sem, later)

    for h in range(2):
        landed(from_prev.at[h], halo_sem.at[h, 0])
    s = scores((from_prev[0], from_prev[1]), (own[0], own[1]))
    s = jnp.where(iota((EDGE, ROWS), 0) - EDGE >= begin, s, -1.0)
    best = jnp.maximum(best, jnp.max(s, axis=0, keepdims=True))
    landed(returned, back_sem)
    back = jnp.concatenate([returned[...], jnp.full((1, ROWS - EDGE), -1.0, f32)], axis=1)
    best_ref[...] = jnp.maximum(best, jnp.where(begin < 0, back, -1.0))

    for h in range(2):
        landed(from_prev.at[h], halo_out.at[h, 0])
        landed(from_next.at[h], halo_out.at[h, 1])
        for g in range(GROUPS):
            for phase in range(2):
                landed(sent0.at[h, g, pl.ds(0, 3)], out_sem.at[h, g, phase])
            landed(unit.at[pl.ds(0, 224)], out_sem.at[h, g, 2])
    landed(returned, back_out)
    landed(meta0.at[pl.ds(0, 3)], mout_sem.at[0])
    landed(meta0.at[pl.ds(0, 3)], mout_sem.at[1])
    landed(flat.at[pl.ds(0, 112)], mout_sem.at[2])


def per_device(embed, cluster, rank, target):
    blocks = (2, GROUPS, 4, 4, 4, 2, 16, 128)
    meta = (4, 4, 4, 2, 1, 128)
    dma = pltpu.SemaphoreType.DMA
    best = pl.pallas_call(
        kernel,
        out_shape=jax.ShapeDtypeStruct((1, ROWS), f32),
        in_specs=[
            pl.BlockSpec(memory_space=pl.ANY),
            pl.BlockSpec(memory_space=pltpu.VMEM),
            pl.BlockSpec(memory_space=pltpu.VMEM),
        ],
        out_specs=pl.BlockSpec(memory_space=pltpu.VMEM),
        scratch_shapes=[
            pltpu.VMEM((ROWS, WIDTH), f32),
            pltpu.VMEM((ROWS, WIDTH), bf16),
            *[pltpu.VMEM(blocks, bf16)] * 4,
            *[pltpu.VMEM(meta, f32)] * 4,
            pltpu.VMEM((DEVICES, 128), f32),
            pltpu.VMEM((GROUPS * 512, HALF), bf16),
            pltpu.VMEM((ROWS, GROUPS * 512), bf16),
            pltpu.VMEM((2, ROWS, HALF), bf16),
            pltpu.VMEM((2, EDGE, HALF), bf16),
            pltpu.VMEM((2, EDGE, HALF), bf16),
            pltpu.VMEM((1, EDGE), f32),
            pltpu.VMEM((1, EDGE), f32),
            dma((3,)),
            dma((2, GROUPS, 4)),
            dma((2, GROUPS, 4)),
            dma((2, GROUPS)),
            dma((2, GROUPS, 3)),
            dma,
            dma,
            dma,
            dma((3,)),
            dma((2, 2)),
            dma((2, 2)),
            dma,
            dma,
        ],
        compiler_params=pltpu.CompilerParams(
            collective_id=0, has_side_effects=True, vmem_limit_bytes=56 * 2**20
        ),
        cost_estimate=pl.CostEstimate(flops=12 * 10**9, bytes_accessed=3 * 2**20, transcendentals=768),
    )(embed, target.reshape(1, ROWS), rank.reshape(1, ROWS))
    return best.reshape(ROWS)


def solution(mesh):
    in_specs = (P(("grp", "sub"), None), P(("grp", "sub")), P(("grp", "sub")), P(("grp", "sub")))
    out_specs = P(("grp", "sub"))
    return jax.shard_map(
        per_device, mesh=mesh, in_specs=in_specs, out_specs=out_specs, check_vma=False
    )
```

```python
import functools

import jax
import jax.numpy as jnp
from jax import lax
from jax.experimental import pallas as pl
from jax.experimental.pallas import tpu as pltpu
from jax.sharding import PartitionSpec as P

MESH = pl.DeviceIdType.MESH
AXES = ("x", "z", "y", "c")
SIZE = {"x": 4, "z": 4, "y": 4, "c": 2}
ORDERS = (("x", "y", "z"), ("y", "z", "x"), ("z", "x", "y"))
ROWS = 768
WIDTH = 1024
HALF = 512
CAP = 12
GROUPS = 3
DEPTH = 4
DEVICES = 128
EDGE = 384
NT = (((1,), (1,)), ((), ()))
bf16, f32, i32 = jnp.bfloat16, jnp.float32, jnp.int32


def view(ref, *lead, **fixed):
    return ref.at[tuple(lead) + tuple(fixed.get(a, slice(None)) for a in AXES)]


def iota(shape, dim):
    return lax.broadcasted_iota(i32, shape, dim)


def dot(a, b, dims=(((1,), (0,)), ((), ())), exact=False):
    precision = lax.Precision.HIGHEST if exact else None
    return lax.dot_general(a, b, dims, precision=precision, preferred_element_type=f32)


def kernel(
    embed_hbm, target_hbm, rank_hbm, best_ref,
    target_ref, rank_ref, embed, unit, sent0, sent1, sent2, sent3, meta0, meta1, meta2, meta3, flat,
    slots, chosen, own, from_prev, from_next, with_prev, with_next, returned, answer,
    load_sem, index_sem, sem1, sem2, sem3, out_sem, msem1, msem2, msem3, mout_sem,
    halo_sem, halo_out, back_sem, back_out,
):
    grp, sub = lax.axis_index("grp"), lax.axis_index("sub")
    me = {"x": grp // 4, "z": lax.rem(grp, 4), "y": sub // 2, "c": lax.rem(sub, 2)}

    def device(**other):
        at = {**me, **other}
        return (at["x"] * 4 + at["z"], at["y"] * 2 + at["c"])

    def around(axis, by):
        return lax.rem(me[axis] + by, 4)

    def remote(src, dst, send_sem, recv_sem, to):
        pltpu.make_async_remote_copy(
            src_ref=src, dst_ref=dst, send_sem=send_sem, recv_sem=recv_sem,
            device_id=to, device_id_type=MESH,
        ).start()

    def landed(ref, sem):
        pltpu.make_async_copy(ref, ref, sem).wait()

    indices = [
        pltpu.make_async_copy(target_hbm, target_ref, index_sem.at[0]),
        pltpu.make_async_copy(rank_hbm, rank_ref, index_sem.at[1]),
    ]
    for load in indices:
        load.start()
    loads = []
    for i in range(3):
        part = pl.ds(i * 256, 256)
        loads.append(pltpu.make_async_copy(embed_hbm.at[part], embed.at[part], load_sem.at[i]))
        loads[-1].start()

    barrier = pltpu.get_barrier_semaphore()
    partners = [device(**{a: around(a, d)}) for a in "xyz" for d in (1, 2, 3)]
    partners += [device(**{a: around(a, d), "c": 1 - me["c"]}) for a in "xyz" for d in (1, 2, 3)]
    partners += [device(c=1 - me["c"])]
    for to in partners:
        pl.semaphore_signal(barrier, inc=1, device_id=to, device_id_type=MESH)

    for load in indices:
        load.wait()
    target = target_ref[...].reshape(1, ROWS).astype(f32)
    rank = rank_ref[...].reshape(1, ROWS).astype(f32)
    owner = jnp.floor((target + 0.5) * (1.0 / ROWS))
    row = target - owner * ROWS
    owns = (owner == iota((DEVICES, ROWS), 0).astype(f32)).astype(f32)
    before = (iota((ROWS, ROWS), 0) < iota((ROWS, ROWS), 1)).astype(f32).astype(bf16)
    count = dot(owns.astype(bf16), before)
    within = jnp.sum(owns * count, axis=0, keepdims=True)
    code = owner * CAP + within
    lane_slot = iota((DEVICES, ROWS), 0).astype(f32)
    spread = jnp.where(within == lane_slot, row + 1.0, 0.0) + jnp.where(
        within + 16.0 == lane_slot, rank, 0.0
    )
    flat[...] = dot(owns, spread, NT, exact=True)
    for x in range(4):
        for z in range(4):
            for y in range(4):
                for c in range(2):
                    at = ((x * 4 + z) * 4 + y) * 2 + c
                    meta0[x, z, y, c] = flat[at : at + 1, :]

    for i in range(3):
        loads[i].wait()

        def normalise(j, _):
            part = pl.ds(pl.multiple_of(i * 256 + j * 64, 64), 64)
            e = embed[part, :]
            squares = jnp.sum(e * e, axis=1, keepdims=True)
            unit[part, :] = (e * lax.rsqrt(squares + 1e-06)).astype(bf16)
            return 0

        lax.fori_loop(0, 4, normalise, 0)

    def meta_first():
        for d in (1, 3, 2):
            t = around("x", d)
            remote(view(meta0, x=t), view(meta1, x=me["x"]), mout_sem.at[0], msem1, device(x=t))
        pltpu.make_async_copy(view(meta0, x=me["x"]), view(meta1, x=me["x"]), msem1).start()

    def meta_second():
        landed(meta1, msem1)
        for d in (1, 3, 2):
            t = around("z", d)
            remote(view(meta1, z=t), view(meta2, z=me["z"]), mout_sem.at[1], msem2, device(z=t))
        pltpu.make_async_copy(view(meta1, z=me["z"]), view(meta2, z=me["z"]), msem2).start()

    def meta_third():
        landed(meta2, msem2)
        for d in (1, 3, 2, 0):
            t = around("y", d)
            for c in (me["c"], 1 - me["c"]):
                if d == 0 and c is me["c"]:
                    continue
                remote(
                    view(meta2, y=t, c=c), view(meta3, y=me["y"], c=me["c"]),
                    mout_sem.at[2], msem3, device(y=t, c=c),
                )
        here = {"y": me["y"], "c": me["c"]}
        pltpu.make_async_copy(view(meta2, **here), view(meta3, **here), msem3).start()

    def pack(h, g):
        k = iota((DEVICES * DEPTH, ROWS), 0)
        wanted = 3 * k - 2 * (k & 3) + DEPTH * g
        pick = (code.astype(i32) == wanted).astype(f32).astype(bf16)
        q = dot(pick, unit[:, h * HALF : (h + 1) * HALF]).reshape(64, 8, HALF)
        r = pltpu.roll(q, 4, 1)
        low = iota((64, 8, 128), 1) < 4
        qs = [q[:, :, 128 * j : 128 * j + 128] for j in range(4)]
        rs = [r[:, :, 128 * j : 128 * j + 128] for j in range(4)]
        even = jnp.concatenate([jnp.where(low, qs[0], rs[1]), jnp.where(low, qs[2], rs[3])], axis=1)
        odd = jnp.concatenate([jnp.where(low, rs[0], qs[1]), jnp.where(low, rs[2], qs[3])], axis=1)
        sent0[h, g, :, :, :, 0] = even.astype(bf16).reshape(4, 4, 4, 16, 128)
        sent0[h, g, :, :, :, 1] = odd.astype(bf16).reshape(4, 4, 4, 16, 128)

    def first(h, g):
        a = ORDERS[g][0]
        for d in (1, 3, 2):
            t = around(a, d)
            remote(
                view(sent0, h, g, **{a: t}), view(sent1, h, g, **{a: me[a]}),
                out_sem.at[h, g, 0], sem1.at[h, g, me[a]], device(**{a: t}),
            )
        here = {a: me[a]}
        pltpu.make_async_copy(
            view(sent0, h, g, **here), view(sent1, h, g, **here), sem1.at[h, g, me[a]]
        ).start()

    def second(h, g, d0):
        a, b, _ = ORDERS[g]
        s = around(a, d0)
        landed(view(sent1, h, g, **{a: s}), sem1.at[h, g, s])
        for d in (1, 3, 2):
            t = around(b, d)
            remote(
                view(sent1, h, g, **{a: s, b: t}), view(sent2, h, g, **{a: s, b: me[b]}),
                out_sem.at[h, g, 1], sem2.at[h, g, me[b]], device(**{b: t}),
            )
        here = {a: s, b: me[b]}
        pltpu.make_async_copy(
            view(sent1, h, g, **here), view(sent2, h, g, **here), sem2.at[h, g, me[b]]
        ).start()

    def third(h, g, d0):
        _, b, e = ORDERS[g]
        s = around(b, d0)
        landed(view(sent2, h, g, **{b: s}), sem2.at[h, g, s])
        for d in (1, 3, 2, 0):
            t = around(e, d)
            for c in (me["c"], 1 - me["c"]):
                if d == 0 and c is me["c"]:
                    continue
                remote(
                    view(sent2, h, g, **{b: s, e: t, "c": c}),
                    view(sent3, h, g, **{b: s, e: me[e], "c": me["c"]}),
                    out_sem.at[h, g, 2], sem3.at[h, g], device(**{e: t, "c": c}),
                )
        here = {b: s, e: me[e], "c": me["c"]}
        pltpu.make_async_copy(
            view(sent2, h, g, **here), view(sent3, h, g, **here), sem3.at[h, g]
        ).start()

    def unpack(h, g):
        landed(sent3.at[h, g], sem3.at[h, g])
        even = sent3[h, g, :, :, :, 0].reshape(64, 16, 128).astype(f32)
        odd = sent3[h, g, :, :, :, 1].reshape(64, 16, 128).astype(f32)
        low = iota((64, 8, 128), 1) < 4
        for j in range(2):
            a, b = even[:, 8 * j : 8 * j + 8], odd[:, 8 * j : 8 * j + 8]
            p = jnp.where(low, a, pltpu.roll(b, 4, 1)).reshape(512, 128)
            q = jnp.where(low, pltpu.roll(a, 4, 1), b).reshape(512, 128)
            slots[h, g * 512 : g * 512 + 512, 256 * j : 256 * j + 128] = p.astype(bf16)
            slots[h, g * 512 : g * 512 + 512, 256 * j + 128 : 256 * j + 256] = q.astype(bf16)

    later = (grp, lax.rem(sub + 1, 8))
    sooner = (grp, lax.rem(sub + 7, 8))

    def gather(h):
        own[h, 0:EDGE, :] = dot(chosen[0:EDGE, :], slots[h]).astype(bf16)
        remote(
            own.at[h, pl.ds(0, EDGE)], from_next.at[h],
            halo_out.at[h, 1], halo_sem.at[h, 1], sooner,
        )
        own[h, EDGE:ROWS, :] = dot(chosen[EDGE:ROWS, :], slots[h]).astype(bf16)
        remote(
            own.at[h, pl.ds(EDGE, EDGE)], from_prev.at[h],
            halo_out.at[h, 0], halo_sem.at[h, 0], later,
        )

    def choose():
        landed(meta3, msem3)
        for x in range(4):
            for z in range(4):
                for y in range(4):
                    for c in range(2):
                        at = ((x * 4 + z) * 4 + y) * 2 + c
                        flat[at : at + 1, :] = meta3[x, z, y, c]
        got = flat[...]
        l, k = iota((128, 768), 0), iota((128, 768), 1)
        g, kind = (k // 128) % 3, k // 384
        expand = (l == kind * 16 + g * DEPTH + (k & 3)).astype(f32)
        wide = dot(got, expand, exact=True)
        mine = (iota((32, 128), 1) >> 2) == iota((32, 128), 0)

        def lanes(first):
            pieces = []
            for g in range(GROUPS):
                for j in range(4):
                    v = wide[32 * j : 32 * j + 32, first + 128 * g : first + 128 * g + 128]
                    pieces.append(jnp.sum(jnp.where(mine, v, 0.0), axis=0, keepdims=True))
            return jnp.concatenate(pieces, axis=1)

        place, its_rank = lanes(0), lanes(384)

        def build(j, _):
            part = pl.ds(pl.multiple_of(j * 64, 64), 64)
            r = (iota((64, 1536), 0) + j * 64 + 1).astype(f32)
            chosen[part, :] = (place == r).astype(f32).astype(bf16)
            return 0

        lax.fori_loop(0, 12, build, 0)
        high = jnp.floor(its_rank * (1.0 / 256.0))
        which = iota((16, 1536), 0)
        both = jnp.where(which == 0, high, jnp.where(which == 1, its_rank - 256.0 * high, 0.0))
        ranks = dot(both.astype(bf16), chosen[...], NT)
        rank_of = ranks[0:1] * 256.0 + ranks[1:2]
        return iota((1, ROWS), 1) - rank_of.astype(i32), rank_of[:, ROWS - 1 : ROWS].astype(i32)

    everyone = range(GROUPS)
    pack(0, 0)
    pl.semaphore_wait(barrier, len(partners))
    meta_first()
    first(0, 0)
    for g in (1, 2):
        pack(0, g)
        first(0, g)
    for g in everyone:
        second(0, g, 0)
    meta_second()
    for g in everyone:
        pack(1, g)
    for d in (1, 3, 2):
        for g in everyone:
            second(0, g, d)
    for g in everyone:
        first(1, g)
    for g in everyone:
        second(1, g, 0)
    meta_third()
    for d in (0, 1, 3, 2):
        for g in everyone:
            third(0, g, d)
    for d in (1, 3, 2):
        for g in everyone:
            second(1, g, d)
    for g in everyone:
        third(1, g, 0)
    begin, last_rank = choose()
    for g in everyone:
        unpack(0, g)
    for d in (1, 3, 2):
        for g in everyone:
            third(1, g, d)
    gather(0)
    for g in everyone:
        unpack(1, g)
    gather(1)

    landed(from_next.at[0], halo_sem.at[0, 1])
    with_next[...] = dot(own[0], from_next[0], NT)
    landed(from_prev.at[0], halo_sem.at[0, 0])
    with_prev[...] = dot(from_prev[0], own[0], NT)

    here = []
    for j in range(3):
        n = 256 * (j + 1)
        p = slice(256 * j, n)
        s = dot(own[0, 0:n], own[0, p], NT) + dot(own[1, 0:n], own[1, p], NT)
        q, at = iota((n, 256), 0), iota((n, 256), 1) + 256 * j
        s = jnp.where((q >= begin[:, p]) & (q < at), s, -1.0)
        here.append(jnp.max(s, axis=0, keepdims=True))
    best = jnp.concatenate(here, axis=1)

    for h in range(2):
        for g in range(GROUPS):
            for phase in range(2):
                landed(sent0.at[h, g, pl.ds(0, 3)], out_sem.at[h, g, phase])
            landed(unit.at[pl.ds(0, 224)], out_sem.at[h, g, 2])
    landed(meta0.at[pl.ds(0, 3)], mout_sem.at[0])
    landed(meta0.at[pl.ds(0, 3)], mout_sem.at[1])
    landed(flat.at[pl.ds(0, 112)], mout_sem.at[2])

    landed(from_next.at[1], halo_sem.at[1, 1])
    s = with_next[...] + dot(own[1], from_next[1], NT)
    s = jnp.where(iota((ROWS, EDGE), 0) >= ROWS - 1 - last_rank, s, -1.0)
    answer[...] = jnp.max(s, axis=0, keepdims=True)
    remote(answer, returned, back_out, back_sem, later)

    landed(from_prev.at[1], halo_sem.at[1, 0])
    s = with_prev[...] + dot(from_prev[1], own[1], NT)
    s = jnp.where(iota((EDGE, ROWS), 0) - EDGE >= begin, s, -1.0)
    best = jnp.maximum(best, jnp.max(s, axis=0, keepdims=True))
    for h in range(2):
        landed(from_prev.at[h], halo_out.at[h, 0])
        landed(from_next.at[h], halo_out.at[h, 1])
    landed(returned, back_sem)
    back = jnp.concatenate([returned[...], jnp.full((1, ROWS - EDGE), -1.0, f32)], axis=1)
    best = jnp.maximum(best, jnp.where(begin < 0, back, -1.0))
    best_ref[...] = best.reshape(ROWS)
    landed(returned, back_out)


def per_device(embed, cluster, rank, target):
    blocks = (2, GROUPS, 4, 4, 4, 2, 16, 128)
    meta = (4, 4, 4, 2, 1, 128)
    dma = pltpu.SemaphoreType.DMA
    best = pl.pallas_call(
        kernel,
        out_shape=pltpu.VMEM((ROWS,), f32),
        in_specs=[
            pl.BlockSpec(memory_space=pl.ANY),
            pl.BlockSpec(memory_space=pl.ANY),
            pl.BlockSpec(memory_space=pl.ANY),
        ],
        out_specs=pl.BlockSpec(memory_space=pltpu.VMEM),
        scratch_shapes=[
            pltpu.VMEM((ROWS,), i32),
            pltpu.VMEM((ROWS,), i32),
            pltpu.VMEM((ROWS, WIDTH), f32),
            pltpu.VMEM((ROWS, WIDTH), bf16),
            *[pltpu.VMEM(blocks, bf16)] * 4,
            *[pltpu.VMEM(meta, f32)] * 4,
            pltpu.VMEM((DEVICES, 128), f32),
            pltpu.VMEM((2, GROUPS * 512, HALF), bf16),
            pltpu.VMEM((ROWS, GROUPS * 512), bf16),
            pltpu.VMEM((2, ROWS, HALF), bf16),
            pltpu.VMEM((2, EDGE, HALF), bf16),
            pltpu.VMEM((2, EDGE, HALF), bf16),
            pltpu.VMEM((EDGE, ROWS), f32),
            pltpu.VMEM((ROWS, EDGE), f32),
            pltpu.VMEM((1, EDGE), f32),
            pltpu.VMEM((1, EDGE), f32),
            dma((3,)),
            dma((2,)),
            dma((2, GROUPS, 4)),
            dma((2, GROUPS, 4)),
            dma((2, GROUPS)),
            dma((2, GROUPS, 3)),
            dma,
            dma,
            dma,
            dma((3,)),
            dma((2, 2)),
            dma((2, 2)),
            dma,
            dma,
        ],
        compiler_params=pltpu.CompilerParams(
            collective_id=0, has_side_effects=True, vmem_limit_bytes=56 * 2**20
        ),
        cost_estimate=pl.CostEstimate(flops=12 * 10**9, bytes_accessed=3 * 2**20, transcendentals=768),
    )(embed, target, rank)
    return best


def solution(mesh):
    in_specs = (P(("grp", "sub"), None), P(("grp", "sub")), P(("grp", "sub")), P(("grp", "sub")))
    out_specs = P(("grp", "sub"))
    return jax.shard_map(
        per_device, mesh=mesh, in_specs=in_specs, out_specs=out_specs, check_vma=False
    )
```

```python
import functools

import jax
import jax.numpy as jnp
from jax import lax
from jax.experimental import pallas as pl
from jax.experimental.pallas import tpu as pltpu
from jax.sharding import PartitionSpec as P

MESH = pl.DeviceIdType.MESH
AXES = ("x", "z", "y", "c")
SIZE = {"x": 4, "z": 4, "y": 4, "c": 2}
ORDERS = (("x", "y", "z"), ("y", "z", "x"), ("z", "x", "y"))
ROWS = 768
WIDTH = 1024
HALF = 512
CAP = 12
GROUPS = 3
DEPTH = 4
DEVICES = 128
EDGE = 352
REST = ROWS - EDGE
NT = (((1,), (1,)), ((), ()))
bf16, f32, i32 = jnp.bfloat16, jnp.float32, jnp.int32


def view(ref, *lead, **fixed):
    return ref.at[tuple(lead) + tuple(fixed.get(a, slice(None)) for a in AXES)]


def iota(shape, dim):
    return lax.broadcasted_iota(i32, shape, dim)


def dot(a, b, dims=(((1,), (0,)), ((), ())), exact=False):
    precision = lax.Precision.HIGHEST if exact else None
    return lax.dot_general(a, b, dims, precision=precision, preferred_element_type=f32)


def kernel(
    embed_hbm, target_hbm, rank_hbm, best_ref,
    target_ref, rank_ref, embed, picks, unit, sent0, sent1, sent2, sent3, meta0, meta1, meta2, meta3, flat,
    slots, chosen, partly, own, from_prev, from_next, with_prev, with_next, returned, answer,
    load_sem, index_sem, sem1, sem2, sem3, out_sem, msem1, msem2, msem3, mout_sem,
    halo_sem, halo_out, back_sem, back_out,
):
    grp, sub = lax.axis_index("grp"), lax.axis_index("sub")
    me = {"x": grp // 4, "z": lax.rem(grp, 4), "y": sub // 2, "c": lax.rem(sub, 2)}

    def device(**other):
        at = {**me, **other}
        return (at["x"] * 4 + at["z"], at["y"] * 2 + at["c"])

    def around(axis, by):
        return lax.rem(me[axis] + by, 4)

    def remote(src, dst, send_sem, recv_sem, to):
        pltpu.make_async_remote_copy(
            src_ref=src, dst_ref=dst, send_sem=send_sem, recv_sem=recv_sem,
            device_id=to, device_id_type=MESH,
        ).start()

    def landed(ref, sem):
        pltpu.make_async_copy(ref, ref, sem).wait()

    indices = [
        pltpu.make_async_copy(target_hbm, target_ref, index_sem.at[0]),
        pltpu.make_async_copy(rank_hbm, rank_ref, index_sem.at[1]),
    ]
    for load in indices:
        load.start()
    loads = []
    for i in range(3):
        part = pl.ds(i * 256, 256)
        loads.append(pltpu.make_async_copy(embed_hbm.at[part], embed.at[part], load_sem.at[i]))
        loads[-1].start()

    barrier = pltpu.get_barrier_semaphore()
    partners = [device(**{a: around(a, d)}) for a in "xyz" for d in (1, 2, 3)]
    partners += [device(**{a: around(a, d), "c": 1 - me["c"]}) for a in "xyz" for d in (1, 2, 3)]
    partners += [device(c=1 - me["c"])]
    for to in partners:
        pl.semaphore_signal(barrier, inc=1, device_id=to, device_id_type=MESH)

    chosen[:, 0:ROWS] = (iota((ROWS, ROWS), 0) < iota((ROWS, ROWS), 1)).astype(f32).astype(bf16)

    for load in indices:
        load.wait()
    target = target_ref[...].reshape(1, ROWS).astype(f32)
    rank = rank_ref[...].reshape(1, ROWS).astype(f32)
    owner = jnp.floor((target + 0.5) * (1.0 / ROWS))
    row = target - owner * ROWS
    owns = (owner == iota((DEVICES, ROWS), 0).astype(f32)).astype(f32)
    count = dot(owns.astype(bf16), chosen[:, 0:ROWS])
    within = jnp.sum(owns * count, axis=0, keepdims=True)
    code = owner * CAP + within
    def pick(g):
        k = iota((DEVICES * DEPTH, ROWS), 0)
        wanted = 3 * k - 2 * (k & 3) + DEPTH * g
        picks[g] = (code.astype(i32) == wanted).astype(f32).astype(bf16)

    pick(1)
    for i in range(3):
        loads[i].wait()

        for j in range(8):
            part = slice(i * 256 + j * 32, i * 256 + j * 32 + 32)
            e = embed[part, :]
            squares = jnp.sum(e * e, axis=1, keepdims=True)
            unit[part, :] = (e * lax.rsqrt(squares + 1e-06)).astype(bf16)

    def meta_first():
        lane_slot = iota((DEVICES, ROWS), 0).astype(f32)
        spread = jnp.where(within == lane_slot, row + 1.0, 0.0) + jnp.where(
            within + 16.0 == lane_slot, rank, 0.0
        )
        flat[...] = dot(owns, spread, NT, exact=True)
        for x in range(4):
            for z in range(4):
                for y in range(4):
                    for c in range(2):
                        at = ((x * 4 + z) * 4 + y) * 2 + c
                        meta0[x, z, y, c] = flat[at : at + 1, :]
        for d in (1, 3, 2):
            t = around("x", d)
            remote(view(meta0, x=t), view(meta1, x=me["x"]), mout_sem.at[0], msem1, device(x=t))
        pltpu.make_async_copy(view(meta0, x=me["x"]), view(meta1, x=me["x"]), msem1).start()

    def meta_second():
        landed(meta1, msem1)
        for d in (1, 3, 2):
            t = around("z", d)
            remote(view(meta1, z=t), view(meta2, z=me["z"]), mout_sem.at[1], msem2, device(z=t))
        pltpu.make_async_copy(view(meta1, z=me["z"]), view(meta2, z=me["z"]), msem2).start()

    def meta_third():
        landed(meta2, msem2)
        for d in (1, 3, 2, 0):
            t = around("y", d)
            for c in (me["c"], 1 - me["c"]):
                if d == 0 and c is me["c"]:
                    continue
                remote(
                    view(meta2, y=t, c=c), view(meta3, y=me["y"], c=me["c"]),
                    mout_sem.at[2], msem3, device(y=t, c=c),
                )
        here = {"y": me["y"], "c": me["c"]}
        pltpu.make_async_copy(view(meta2, **here), view(meta3, **here), msem3).start()

    def pack(h, g):
        q = dot(picks[g], unit[:, h * HALF : (h + 1) * HALF]).reshape(64, 8, HALF)
        r = pltpu.roll(q, 4, 1)
        low = iota((64, 8, 128), 1) < 4
        qs = [q[:, :, 128 * j : 128 * j + 128] for j in range(4)]
        rs = [r[:, :, 128 * j : 128 * j + 128] for j in range(4)]
        even = jnp.concatenate([jnp.where(low, qs[0], rs[1]), jnp.where(low, qs[2], rs[3])], axis=1)
        odd = jnp.concatenate([jnp.where(low, rs[0], qs[1]), jnp.where(low, rs[2], qs[3])], axis=1)
        sent0[h, g, :, :, :, 0] = even.astype(bf16).reshape(4, 4, 4, 16, 128)
        sent0[h, g, :, :, :, 1] = odd.astype(bf16).reshape(4, 4, 4, 16, 128)

    def first(h, g):
        a = ORDERS[g][0]
        for d in (1, 3, 2):
            t = around(a, d)
            remote(
                view(sent0, h, g, **{a: t}), view(sent1, h, g, **{a: me[a]}),
                out_sem.at[h, g, 0], sem1.at[h, g, me[a]], device(**{a: t}),
            )
        here = {a: me[a]}
        pltpu.make_async_copy(
            view(sent0, h, g, **here), view(sent1, h, g, **here), sem1.at[h, g, me[a]]
        ).start()

    def second(h, g, d0):
        a, b, _ = ORDERS[g]
        s = around(a, d0)
        landed(view(sent1, h, g, **{a: s}), sem1.at[h, g, s])
        for d in (1, 3, 2):
            t = around(b, d)
            remote(
                view(sent1, h, g, **{a: s, b: t}), view(sent2, h, g, **{a: s, b: me[b]}),
                out_sem.at[h, g, 1], sem2.at[h, g, me[b]], device(**{b: t}),
            )
        here = {a: s, b: me[b]}
        pltpu.make_async_copy(
            view(sent1, h, g, **here), view(sent2, h, g, **here), sem2.at[h, g, me[b]]
        ).start()

    def third(h, g, d0):
        _, b, e = ORDERS[g]
        s = around(b, d0)
        landed(view(sent2, h, g, **{b: s}), sem2.at[h, g, s])
        for d in (1, 3, 2, 0):
            t = around(e, d)
            for c in (me["c"], 1 - me["c"]):
                if d == 0 and c is me["c"]:
                    continue
                remote(
                    view(sent2, h, g, **{b: s, e: t, "c": c}),
                    view(sent3, h, g, **{b: s, e: me[e], "c": me["c"]}),
                    out_sem.at[h, g, 2], sem3.at[h, g], device(**{e: t, "c": c}),
                )
        here = {b: s, e: me[e], "c": me["c"]}
        pltpu.make_async_copy(
            view(sent2, h, g, **here), view(sent3, h, g, **here), sem3.at[h, g]
        ).start()

    def unpack(h, g):
        landed(sent3.at[h, g], sem3.at[h, g])
        even = sent3[h, g, :, :, :, 0].reshape(64, 16, 128).astype(f32)
        odd = sent3[h, g, :, :, :, 1].reshape(64, 16, 128).astype(f32)
        low = iota((64, 8, 128), 1) < 4
        rows = pl.ds(pl.multiple_of(g * 512, 512), 512)
        for j in range(2):
            a, b = even[:, 8 * j : 8 * j + 8], odd[:, 8 * j : 8 * j + 8]
            p = jnp.where(low, a, pltpu.roll(b, 4, 1)).reshape(512, 128)
            q = jnp.where(low, pltpu.roll(a, 4, 1), b).reshape(512, 128)
            slots[h, rows, 256 * j : 256 * j + 128] = p.astype(bf16)
            slots[h, rows, 256 * j + 128 : 256 * j + 256] = q.astype(bf16)

    later = (grp, lax.rem(sub + 1, 8))
    sooner = (grp, lax.rem(sub + 7, 8))

    def halo_sooner(h):
        remote(
            own.at[h, pl.ds(0, EDGE)], from_next.at[h],
            halo_out.at[h, 1], halo_sem.at[h, 1], sooner,
        )

    def halo_later(h):
        remote(
            own.at[h, pl.ds(EDGE, REST)], from_prev.at[h],
            halo_out.at[h, 0], halo_sem.at[h, 0], later,
        )

    def gather():
        own[0, 0:EDGE, :] = dot(chosen[0:EDGE, :], slots[0]).astype(bf16)
        halo_sooner(0)
        own[0, EDGE:ROWS, :] = dot(chosen[EDGE:ROWS, :], slots[0]).astype(bf16)
        halo_later(0)

    def gather_most():
        partly[...] = dot(chosen[:, 0:1024], slots[1, 0:1024])

    def gather_rest():
        for part in (slice(0, EDGE), slice(EDGE, ROWS)):
            rest = dot(chosen[part, 1024:1536], slots[1, 1024:1536])
            own[1, part, :] = (partly[part, :] + rest).astype(bf16)
            if part.start == 0:
                halo_sooner(1)
            else:
                halo_later(1)

    def choose():
        landed(meta3, msem3)
        for x in range(4):
            for z in range(4):
                for y in range(4):
                    for c in range(2):
                        at = ((x * 4 + z) * 4 + y) * 2 + c
                        flat[at : at + 1, :] = meta3[x, z, y, c]
        got = flat[...]
        l, k = iota((128, 768), 0), iota((128, 768), 1)
        g, kind = (k // 128) % 3, k // 384
        expand = (l == kind * 16 + g * DEPTH + (k & 3)).astype(f32)
        wide = dot(got, expand, exact=True)
        mine = (iota((32, 128), 1) >> 2) == iota((32, 128), 0)

        def lanes(first):
            pieces = []
            for g in range(GROUPS):
                for j in range(4):
                    v = wide[32 * j : 32 * j + 32, first + 128 * g : first + 128 * g + 128]
                    pieces.append(jnp.sum(jnp.where(mine, v, 0.0), axis=0, keepdims=True))
            return jnp.concatenate(pieces, axis=1)

        place, its_rank = lanes(0), lanes(384)

        def build(j, _):
            part = pl.ds(pl.multiple_of(j * 64, 64), 64)
            r = (iota((64, 1536), 0) + j * 64 + 1).astype(f32)
            chosen[part, :] = (place == r).astype(f32).astype(bf16)
            return 0

        lax.fori_loop(0, 12, build, 0)
        high = jnp.floor(its_rank * (1.0 / 256.0))
        which = iota((16, 1536), 0)
        both = jnp.where(which == 0, high, jnp.where(which == 1, its_rank - 256.0 * high, 0.0))
        ranks = dot(both.astype(bf16), chosen[...], NT)
        rank_of = ranks[0:1] * 256.0 + ranks[1:2]
        return iota((1, ROWS), 1) - rank_of.astype(i32), rank_of[:, ROWS - 1 : ROWS].astype(i32)

    everyone = range(GROUPS)

    def repeat(step):
        def once(g, _):
            step(g)
            return 0

        lax.fori_loop(0, GROUPS, once, 0)

    pack(0, 1)
    pl.semaphore_wait(barrier, len(partners))
    first(0, 1)
    pick(0)
    pack(0, 0)
    first(0, 0)
    second(0, 0, 0)
    pick(2)
    pack(0, 2)
    first(0, 2)
    second(0, 1, 0)
    second(0, 2, 0)
    meta_first()
    pack(1, 1)
    first(1, 1)
    for d in (1, 3, 2):
        for g in everyone:
            second(0, g, d)
    pack(1, 0)
    first(1, 0)
    second(1, 0, 0)
    pack(1, 2)
    first(1, 2)
    second(1, 1, 0)
    second(1, 2, 0)
    meta_second()
    for d in (0, 1, 3, 2):
        for g in (2, 0, 1):
            third(0, g, d)
    meta_third()
    for d in (1, 3, 2):
        for g in everyone:
            second(1, g, d)
    for g in (2, 0, 1):
        third(1, g, 0)
    for d in (1, 3, 2):
        for g in (2, 0, 1):
            third(1, g, d)
    begin, last_rank = choose()
    repeat(lambda g: unpack(0, g))
    gather()
    unpack(1, 0)
    unpack(1, 1)
    gather_most()
    unpack(1, 2)
    gather_rest()

    landed(from_next.at[0], halo_sem.at[0, 1])
    with_next[...] = dot(own[0], from_next[0], NT)
    landed(from_prev.at[0], halo_sem.at[0, 0])
    with_prev[...] = dot(from_prev[0], own[0], NT)

    here = []
    for j in range(3):
        n = 256 * (j + 1)
        p = slice(256 * j, n)
        s = dot(own[0, 0:n], own[0, p], NT) + dot(own[1, 0:n], own[1, p], NT)
        q, at = iota((n, 256), 0), iota((n, 256), 1) + 256 * j
        s = jnp.where((q >= begin[:, p]) & (q < at), s, -1.0)
        here.append(jnp.max(s, axis=0, keepdims=True))
    best = jnp.concatenate(here, axis=1)

    for h in range(2):
        for g in range(GROUPS):
            for phase in range(2):
                landed(sent0.at[h, g, pl.ds(0, 3)], out_sem.at[h, g, phase])
            landed(unit.at[pl.ds(0, 224)], out_sem.at[h, g, 2])
    landed(meta0.at[pl.ds(0, 3)], mout_sem.at[0])
    landed(meta0.at[pl.ds(0, 3)], mout_sem.at[1])
    landed(flat.at[pl.ds(0, 112)], mout_sem.at[2])

    landed(from_next.at[1], halo_sem.at[1, 1])
    s = with_next[...] + dot(own[1], from_next[1], NT)
    s = jnp.where(iota((ROWS, EDGE), 0) >= ROWS - 1 - last_rank, s, -1.0)
    answer[...] = jnp.max(s, axis=0, keepdims=True)
    remote(answer, returned, back_out, back_sem, later)

    landed(from_prev.at[1], halo_sem.at[1, 0])
    s = with_prev[...] + dot(from_prev[1], own[1], NT)
    s = jnp.where(iota((REST, ROWS), 0) - REST >= begin, s, -1.0)
    best = jnp.maximum(best, jnp.max(s, axis=0, keepdims=True))
    for h in range(2):
        landed(from_prev.at[h], halo_out.at[h, 0])
        landed(from_next.at[h], halo_out.at[h, 1])
    landed(returned, back_sem)
    back = jnp.concatenate([returned[...], jnp.full((1, ROWS - EDGE), -1.0, f32)], axis=1)
    best = jnp.maximum(best, jnp.where(begin < 0, back, -1.0))
    best_ref[...] = best.reshape(ROWS)
    landed(returned, back_out)


def per_device(embed, cluster, rank, target):
    blocks = (2, GROUPS, 4, 4, 4, 2, 16, 128)
    meta = (4, 4, 4, 2, 1, 128)
    dma = pltpu.SemaphoreType.DMA
    best = pl.pallas_call(
        kernel,
        out_shape=pltpu.VMEM((ROWS,), f32),
        in_specs=[
            pl.BlockSpec(memory_space=pl.ANY),
            pl.BlockSpec(memory_space=pl.ANY),
            pl.BlockSpec(memory_space=pl.ANY),
        ],
        out_specs=pl.BlockSpec(memory_space=pltpu.VMEM),
        scratch_shapes=[
            pltpu.VMEM((ROWS,), i32),
            pltpu.VMEM((ROWS,), i32),
            pltpu.VMEM((ROWS, WIDTH), f32),
            pltpu.VMEM((GROUPS, DEVICES * DEPTH, ROWS), bf16),
            pltpu.VMEM((ROWS, WIDTH), bf16),
            *[pltpu.VMEM(blocks, bf16)] * 4,
            *[pltpu.VMEM(meta, f32)] * 4,
            pltpu.VMEM((DEVICES, 128), f32),
            pltpu.VMEM((2, GROUPS * 512, HALF), bf16),
            pltpu.VMEM((ROWS, GROUPS * 512), bf16),
            pltpu.VMEM((ROWS, HALF), f32),
            pltpu.VMEM((2, ROWS, HALF), bf16),
            pltpu.VMEM((2, REST, HALF), bf16),
            pltpu.VMEM((2, EDGE, HALF), bf16),
            pltpu.VMEM((REST, ROWS), f32),
            pltpu.VMEM((ROWS, EDGE), f32),
            pltpu.VMEM((1, EDGE), f32),
            pltpu.VMEM((1, EDGE), f32),
            dma((3,)),
            dma((2,)),
            dma((2, GROUPS, 4)),
            dma((2, GROUPS, 4)),
            dma((2, GROUPS)),
            dma((2, GROUPS, 3)),
            dma,
            dma,
            dma,
            dma((3,)),
            dma((2, 2)),
            dma((2, 2)),
            dma,
            dma,
        ],
        compiler_params=pltpu.CompilerParams(
            collective_id=0, has_side_effects=True, vmem_limit_bytes=56 * 2**20
        ),
        cost_estimate=pl.CostEstimate(flops=12 * 10**9, bytes_accessed=3 * 2**20, transcendentals=768),
    )(embed, target, rank)
    return best


def solution(mesh):
    in_specs = (P(("grp", "sub"), None), P(("grp", "sub")), P(("grp", "sub")), P(("grp", "sub")))
    out_specs = P(("grp", "sub"))
    return jax.shard_map(
        per_device, mesh=mesh, in_specs=in_specs, out_specs=out_specs, check_vma=False
    )
```

```python
import functools

import jax
import jax.numpy as jnp
from jax import lax
from jax.experimental import pallas as pl
from jax.experimental.pallas import tpu as pltpu
from jax.sharding import PartitionSpec as P

MESH = pl.DeviceIdType.MESH
AXES = ("x", "z", "y", "c")
SIZE = {"x": 4, "z": 4, "y": 4, "c": 2}
ORDERS = (("x", "y", "z"), ("y", "z", "x"), ("z", "x", "y"))
ROWS = 768
WIDTH = 1024
HALF = 512
CAP = 12
GROUPS = 3
DEPTH = 4
DEVICES = 128
EDGE = 336
REST = ROWS - EDGE
PARTS = ((0, 256), (256, EDGE), (EDGE, EDGE + 256), (EDGE + 256, ROWS))
NT = (((1,), (1,)), ((), ()))
bf16, f32, i32 = jnp.bfloat16, jnp.float32, jnp.int32


def view(ref, *lead, **fixed):
    return ref.at[tuple(lead) + tuple(fixed.get(a, slice(None)) for a in AXES)]


def iota(shape, dim):
    return lax.broadcasted_iota(i32, shape, dim)


def dot(a, b, dims=(((1,), (0,)), ((), ())), exact=False):
    precision = lax.Precision.HIGHEST if exact else None
    return lax.dot_general(a, b, dims, precision=precision, preferred_element_type=f32)


def kernel(
    embed_hbm, target_hbm, rank_hbm, best_ref,
    target_ref, rank_ref, embed, scale, picks, unit, sent0, sent1, sent2, sent3, meta0, meta1, meta2, meta3, flat,
    slots, chosen, partly, own, from_prev, from_next, with_prev, with_next, returned, answer,
    load_sem, index_sem, sem1, sem2, sem3, out_sem, msem1, msem2, msem3, mout_sem,
    halo_sem, halo_out, last_sem, last_out, back_sem, back_out,
):
    grp, sub = lax.axis_index("grp"), lax.axis_index("sub")
    me = {"x": grp // 4, "z": lax.rem(grp, 4), "y": sub // 2, "c": lax.rem(sub, 2)}

    def device(**other):
        at = {**me, **other}
        return (at["x"] * 4 + at["z"], at["y"] * 2 + at["c"])

    def around(axis, by):
        return lax.rem(me[axis] + by, 4)

    def remote(src, dst, send_sem, recv_sem, to):
        pltpu.make_async_remote_copy(
            src_ref=src, dst_ref=dst, send_sem=send_sem, recv_sem=recv_sem,
            device_id=to, device_id_type=MESH,
        ).start()

    def landed(ref, sem):
        pltpu.make_async_copy(ref, ref, sem).wait()

    indices = [
        pltpu.make_async_copy(target_hbm, target_ref, index_sem.at[0]),
        pltpu.make_async_copy(rank_hbm, rank_ref, index_sem.at[1]),
    ]
    for load in indices:
        load.start()
    loads = []
    for i in range(3):
        part = pl.ds(i * 256, 256)
        loads.append(pltpu.make_async_copy(embed_hbm.at[part], embed.at[part], load_sem.at[i]))
        loads[-1].start()

    barrier = pltpu.get_barrier_semaphore()
    partners = [device(**{a: around(a, d)}) for a in "xyz" for d in (1, 2, 3)]
    partners += [device(**{a: around(a, d), "c": 1 - me["c"]}) for a in "xyz" for d in (1, 2, 3)]
    partners += [device(c=1 - me["c"])]
    for to in partners:
        pl.semaphore_signal(barrier, inc=1, device_id=to, device_id_type=MESH)

    chosen[:, 0:ROWS] = (iota((ROWS, ROWS), 0) < iota((ROWS, ROWS), 1)).astype(f32).astype(bf16)

    for load in indices:
        load.wait()
    target = target_ref[...].reshape(1, ROWS).astype(f32)
    rank = rank_ref[...].reshape(1, ROWS).astype(f32)
    owner = jnp.floor((target + 0.5) * (1.0 / ROWS))
    row = target - owner * ROWS
    owns = (owner == iota((DEVICES, ROWS), 0).astype(f32)).astype(f32)
    count = dot(owns.astype(bf16), chosen[:, 0:ROWS])
    within = jnp.sum(owns * count, axis=0, keepdims=True)
    code = owner * CAP + within
    def pick(g):
        k = iota((DEVICES * DEPTH, ROWS), 0)
        wanted = 3 * k - 2 * (k & 3) + DEPTH * g
        picks[g] = (code.astype(i32) == wanted).astype(f32).astype(bf16)

    pick(1)
    for i in range(3):
        loads[i].wait()

        for j in range(8):
            part = slice(i * 256 + j * 32, i * 256 + j * 32 + 32)
            e = embed[part, :]
            squares = jnp.sum(e * e, axis=1, keepdims=True)
            scale[part, :] = jnp.broadcast_to(lax.rsqrt(squares + 1e-06), (32, 128))
            unit[part, 0:HALF] = (e[:, 0:HALF] * jnp.tile(scale[part, :], (1, 4))).astype(bf16)

    def meta_first():
        lane_slot = iota((DEVICES, ROWS), 0).astype(f32)
        spread = jnp.where(within == lane_slot, row + 1.0, 0.0) + jnp.where(
            within + 16.0 == lane_slot, rank, 0.0
        )
        flat[...] = dot(owns, spread, NT, exact=True)
        for x in range(4):
            for z in range(4):
                for y in range(4):
                    for c in range(2):
                        at = ((x * 4 + z) * 4 + y) * 2 + c
                        meta0[x, z, y, c] = flat[at : at + 1, :]
        for d in (1, 3, 2):
            t = around("x", d)
            remote(view(meta0, x=t), view(meta1, x=me["x"]), mout_sem.at[0], msem1, device(x=t))
        pltpu.make_async_copy(view(meta0, x=me["x"]), view(meta1, x=me["x"]), msem1).start()

    def meta_second():
        landed(meta1, msem1)
        for d in (1, 3, 2):
            t = around("z", d)
            remote(view(meta1, z=t), view(meta2, z=me["z"]), mout_sem.at[1], msem2, device(z=t))
        pltpu.make_async_copy(view(meta1, z=me["z"]), view(meta2, z=me["z"]), msem2).start()

    def meta_third():
        landed(meta2, msem2)
        for d in (1, 3, 2, 0):
            t = around("y", d)
            for c in (me["c"], 1 - me["c"]):
                if d == 0 and c is me["c"]:
                    continue
                remote(
                    view(meta2, y=t, c=c), view(meta3, y=me["y"], c=me["c"]),
                    mout_sem.at[2], msem3, device(y=t, c=c),
                )
        here = {"y": me["y"], "c": me["c"]}
        pltpu.make_async_copy(view(meta2, **here), view(meta3, **here), msem3).start()

    def pack(h, g):
        q = dot(picks[g], unit[:, h * HALF : (h + 1) * HALF]).reshape(64, 8, HALF)
        r = pltpu.roll(q, 4, 1)
        low = iota((64, 8, 128), 1) < 4
        qs = [q[:, :, 128 * j : 128 * j + 128] for j in range(4)]
        rs = [r[:, :, 128 * j : 128 * j + 128] for j in range(4)]
        even = jnp.concatenate([jnp.where(low, qs[0], rs[1]), jnp.where(low, qs[2], rs[3])], axis=1)
        odd = jnp.concatenate([jnp.where(low, rs[0], qs[1]), jnp.where(low, rs[2], qs[3])], axis=1)
        sent0[h, g, :, :, :, 0] = even.astype(bf16).reshape(4, 4, 4, 16, 128)
        sent0[h, g, :, :, :, 1] = odd.astype(bf16).reshape(4, 4, 4, 16, 128)

    def first(h, g):
        a = ORDERS[g][0]
        for d in (1, 3, 2):
            t = around(a, d)
            remote(
                view(sent0, h, g, **{a: t}), view(sent1, h, g, **{a: me[a]}),
                out_sem.at[h, g, 0], sem1.at[h, g, me[a]], device(**{a: t}),
            )
        here = {a: me[a]}
        pltpu.make_async_copy(
            view(sent0, h, g, **here), view(sent1, h, g, **here), sem1.at[h, g, me[a]]
        ).start()

    def second(h, g, d0):
        a, b, _ = ORDERS[g]
        s = around(a, d0)
        landed(view(sent1, h, g, **{a: s}), sem1.at[h, g, s])
        for d in (1, 3, 2):
            t = around(b, d)
            remote(
                view(sent1, h, g, **{a: s, b: t}), view(sent2, h, g, **{a: s, b: me[b]}),
                out_sem.at[h, g, 1], sem2.at[h, g, me[b]], device(**{b: t}),
            )
        here = {a: s, b: me[b]}
        pltpu.make_async_copy(
            view(sent1, h, g, **here), view(sent2, h, g, **here), sem2.at[h, g, me[b]]
        ).start()

    def third(h, g, d0):
        _, b, e = ORDERS[g]
        s = around(b, d0)
        landed(view(sent2, h, g, **{b: s}), sem2.at[h, g, s])
        for d in (1, 3, 2, 0):
            t = around(e, d)
            for c in (me["c"], 1 - me["c"]):
                if d == 0 and c is me["c"]:
                    continue
                remote(
                    view(sent2, h, g, **{b: s, e: t, "c": c}),
                    view(sent3, h, g, **{b: s, e: me[e], "c": me["c"]}),
                    out_sem.at[h, g, 2], sem3.at[h, g], device(**{e: t, "c": c}),
                )
        here = {b: s, e: me[e], "c": me["c"]}
        pltpu.make_async_copy(
            view(sent2, h, g, **here), view(sent3, h, g, **here), sem3.at[h, g]
        ).start()

    def unpack(h, g):
        landed(sent3.at[h, g], sem3.at[h, g])
        even = sent3[h, g, :, :, :, 0].reshape(64, 16, 128).astype(f32)
        odd = sent3[h, g, :, :, :, 1].reshape(64, 16, 128).astype(f32)
        low = iota((64, 8, 128), 1) < 4
        rows = pl.ds(pl.multiple_of(g * 512, 512), 512)
        for j in range(2):
            a, b = even[:, 8 * j : 8 * j + 8], odd[:, 8 * j : 8 * j + 8]
            p = jnp.where(low, a, pltpu.roll(b, 4, 1)).reshape(512, 128)
            q = jnp.where(low, pltpu.roll(a, 4, 1), b).reshape(512, 128)
            slots[h, rows, 256 * j : 256 * j + 128] = p.astype(bf16)
            slots[h, rows, 256 * j + 128 : 256 * j + 256] = q.astype(bf16)

    later = (grp, lax.rem(sub + 1, 8))
    sooner = (grp, lax.rem(sub + 7, 8))

    def halo_sooner(h):
        remote(
            own.at[h, pl.ds(0, EDGE)], from_next.at[h],
            halo_out.at[1], halo_sem.at[1], sooner,
        )

    def halo_later(h):
        remote(
            own.at[h, pl.ds(EDGE, REST)], from_prev.at[h],
            halo_out.at[0], halo_sem.at[0], later,
        )

    def gather():
        own[0, 0:EDGE, :] = dot(chosen[0:EDGE, :], slots[0]).astype(bf16)
        halo_sooner(0)
        own[0, EDGE:ROWS, :] = dot(chosen[EDGE:ROWS, :], slots[0]).astype(bf16)
        halo_later(0)

    def gather_most():
        partly[...] = dot(chosen[:, 0:1024], slots[1, 0:1024])

    def gather_rest():
        for i, (lo, hi) in enumerate(PARTS):
            rest = dot(chosen[lo:hi, 1024:1536], slots[1, 1024:1536])
            own[1, lo:hi, :] = (partly[lo:hi, :] + rest).astype(bf16)
            if hi <= EDGE:
                there, to = from_next.at[1, pl.ds(lo, hi - lo)], sooner
            else:
                there, to = from_prev.at[1, pl.ds(lo - EDGE, hi - lo)], later
            remote(own.at[1, pl.ds(lo, hi - lo)], there, last_out.at[i], last_sem.at[i], to)

    def choose():
        landed(meta3, msem3)
        for x in range(4):
            for z in range(4):
                for y in range(4):
                    for c in range(2):
                        at = ((x * 4 + z) * 4 + y) * 2 + c
                        flat[at : at + 1, :] = meta3[x, z, y, c]
        got = flat[...]
        l, k = iota((128, 768), 0), iota((128, 768), 1)
        g, kind = (k // 128) % 3, k // 384
        expand = (l == kind * 16 + g * DEPTH + (k & 3)).astype(f32)
        wide = dot(got, expand, exact=True)
        mine = (iota((32, 128), 1) >> 2) == iota((32, 128), 0)

        def lanes(first):
            pieces = []
            for g in range(GROUPS):
                for j in range(4):
                    v = wide[32 * j : 32 * j + 32, first + 128 * g : first + 128 * g + 128]
                    pieces.append(jnp.sum(jnp.where(mine, v, 0.0), axis=0, keepdims=True))
            return jnp.concatenate(pieces, axis=1)

        place, its_rank = lanes(0), lanes(384)

        def build(j, _):
            part = pl.ds(pl.multiple_of(j * 64, 64), 64)
            r = (iota((64, 1536), 0) + j * 64 + 1).astype(f32)
            chosen[part, :] = (place == r).astype(f32).astype(bf16)
            return 0

        lax.fori_loop(0, 12, build, 0)
        high = jnp.floor(its_rank * (1.0 / 256.0))
        which = iota((16, 1536), 0)
        both = jnp.where(which == 0, high, jnp.where(which == 1, its_rank - 256.0 * high, 0.0))
        ranks = dot(both.astype(bf16), chosen[...], NT)
        rank_of = ranks[0:1] * 256.0 + ranks[1:2]
        return iota((1, ROWS), 1) - rank_of.astype(i32), rank_of[:, ROWS - 1 : ROWS].astype(i32)

    everyone = range(GROUPS)

    def repeat(step):
        def once(g, _):
            step(g)
            return 0

        lax.fori_loop(0, GROUPS, once, 0)

    pack(0, 1)
    pl.semaphore_wait(barrier, len(partners))
    first(0, 1)
    second(0, 1, 0)
    pick(0)
    pack(0, 0)
    first(0, 0)
    second(0, 0, 0)
    pick(2)
    pack(0, 2)
    first(0, 2)
    second(0, 2, 0)
    meta_first()

    def other_half(i, _):
        part = pl.ds(pl.multiple_of(i * 64, 64), 64)
        e = embed[part, HALF:WIDTH]
        unit[part, HALF:WIDTH] = (e * jnp.tile(scale[part, :], (1, 4))).astype(bf16)
        return 0

    lax.fori_loop(0, 12, other_half, 0)
    pack(1, 1)
    first(1, 1)
    for d in (1, 3, 2):
        for g in everyone:
            second(0, g, d)
    pack(1, 0)
    first(1, 0)
    second(1, 0, 0)
    pack(1, 2)
    first(1, 2)
    second(1, 1, 0)
    second(1, 2, 0)
    meta_second()
    for d in (0, 1, 3, 2):
        for g in (2, 0, 1):
            third(0, g, d)
    meta_third()
    for d in (1, 3, 2):
        for g in everyone:
            second(1, g, d)
    for g in (2, 0, 1):
        third(1, g, 0)
    for d in (1, 3, 2):
        for g in (2, 0, 1):
            third(1, g, d)
    begin, last_rank = choose()
    repeat(lambda g: unpack(0, g))
    gather()
    unpack(1, 0)
    unpack(1, 1)
    gather_most()
    unpack(1, 2)
    gather_rest()

    landed(from_next.at[0], halo_sem.at[1])
    with_next[...] = dot(own[0], from_next[0], NT)
    landed(from_prev.at[0], halo_sem.at[0])
    with_prev[...] = dot(from_prev[0], own[0], NT)

    here = []
    for j in range(3):
        n = 256 * (j + 1)
        p = slice(256 * j, n)
        s = dot(own[0, 0:n], own[0, p], NT) + dot(own[1, 0:n], own[1, p], NT)
        q, at = iota((n, 256), 0), iota((n, 256), 1) + 256 * j
        s = jnp.where((q >= begin[:, p]) & (q < at), s, -1.0)
        here.append(jnp.max(s, axis=0, keepdims=True))
    best = jnp.concatenate(here, axis=1)

    for h in range(2):
        for g in range(GROUPS):
            for phase in range(2):
                landed(sent0.at[h, g, pl.ds(0, 3)], out_sem.at[h, g, phase])
            landed(unit.at[pl.ds(0, 224)], out_sem.at[h, g, 2])
    landed(meta0.at[pl.ds(0, 3)], mout_sem.at[0])
    landed(meta0.at[pl.ds(0, 3)], mout_sem.at[1])
    landed(flat.at[pl.ds(0, 112)], mout_sem.at[2])

    for i, (lo, hi) in enumerate(PARTS[:2]):
        landed(from_next.at[1, pl.ds(lo, hi - lo)], last_sem.at[i])
        s = with_next[:, lo:hi] + dot(own[1], from_next[1, lo:hi], NT)
        s = jnp.where(iota((ROWS, hi - lo), 0) >= ROWS - 1 - last_rank, s, -1.0)
        answer[:, lo:hi] = jnp.max(s, axis=0, keepdims=True)
    remote(answer, returned, back_out, back_sem, later)

    for i, (lo, hi) in enumerate(PARTS[2:]):
        lo, hi = lo - EDGE, hi - EDGE
        landed(from_prev.at[1, pl.ds(lo, hi - lo)], last_sem.at[2 + i])
        s = with_prev[lo:hi, :] + dot(from_prev[1, lo:hi], own[1], NT)
        s = jnp.where(iota((hi - lo, ROWS), 0) + (lo - REST) >= begin, s, -1.0)
        best = jnp.maximum(best, jnp.max(s, axis=0, keepdims=True))
    landed(from_prev.at[0], halo_out.at[0])
    landed(from_next.at[0], halo_out.at[1])
    for i, (lo, hi) in enumerate(PARTS):
        landed(own.at[1, pl.ds(lo, hi - lo)], last_out.at[i])
    landed(returned, back_sem)
    back = jnp.concatenate([returned[...], jnp.full((1, ROWS - EDGE), -1.0, f32)], axis=1)
    best = jnp.maximum(best, jnp.where(begin < 0, back, -1.0))
    best_ref[...] = best.reshape(ROWS)
    landed(returned, back_out)


def per_device(embed, cluster, rank, target):
    blocks = (2, GROUPS, 4, 4, 4, 2, 16, 128)
    meta = (4, 4, 4, 2, 1, 128)
    dma = pltpu.SemaphoreType.DMA
    best = pl.pallas_call(
        kernel,
        out_shape=pltpu.VMEM((ROWS,), f32),
        in_specs=[
            pl.BlockSpec(memory_space=pl.ANY),
            pl.BlockSpec(memory_space=pl.ANY),
            pl.BlockSpec(memory_space=pl.ANY),
        ],
        out_specs=pl.BlockSpec(memory_space=pltpu.VMEM),
        scratch_shapes=[
            pltpu.VMEM((ROWS,), i32),
            pltpu.VMEM((ROWS,), i32),
            pltpu.VMEM((ROWS, WIDTH), f32),
            pltpu.VMEM((ROWS, 128), f32),
            pltpu.VMEM((GROUPS, DEVICES * DEPTH, ROWS), bf16),
            pltpu.VMEM((ROWS, WIDTH), bf16),
            *[pltpu.VMEM(blocks, bf16)] * 4,
            *[pltpu.VMEM(meta, f32)] * 4,
            pltpu.VMEM((DEVICES, 128), f32),
            pltpu.VMEM((2, GROUPS * 512, HALF), bf16),
            pltpu.VMEM((ROWS, GROUPS * 512), bf16),
            pltpu.VMEM((ROWS, HALF), f32),
            pltpu.VMEM((2, ROWS, HALF), bf16),
            pltpu.VMEM((2, REST, HALF), bf16),
            pltpu.VMEM((2, EDGE, HALF), bf16),
            pltpu.VMEM((REST, ROWS), f32),
            pltpu.VMEM((ROWS, EDGE), f32),
            pltpu.VMEM((1, EDGE), f32),
            pltpu.VMEM((1, EDGE), f32),
            dma((3,)),
            dma((2,)),
            dma((2, GROUPS, 4)),
            dma((2, GROUPS, 4)),
            dma((2, GROUPS)),
            dma((2, GROUPS, 3)),
            dma,
            dma,
            dma,
            dma((3,)),
            dma((2,)),
            dma((2,)),
            dma((4,)),
            dma((4,)),
            dma,
            dma,
        ],
        compiler_params=pltpu.CompilerParams(
            collective_id=0, has_side_effects=True, vmem_limit_bytes=56 * 2**20
        ),
        cost_estimate=pl.CostEstimate(flops=12 * 10**9, bytes_accessed=3 * 2**20, transcendentals=768),
    )(embed, target, rank)
    return best


def solution(mesh):
    in_specs = (P(("grp", "sub"), None), P(("grp", "sub")), P(("grp", "sub")), P(("grp", "sub")))
    out_specs = P(("grp", "sub"))
    return jax.shard_map(
        per_device, mesh=mesh, in_specs=in_specs, out_specs=out_specs, check_vma=False
    )
```

```python
import functools

import jax
import jax.numpy as jnp
from jax import lax
from jax.experimental import pallas as pl
from jax.experimental.pallas import tpu as pltpu
from jax.sharding import PartitionSpec as P

MESH = pl.DeviceIdType.MESH
AXES = ("x", "z", "y", "c")
SIZE = {"x": 4, "z": 4, "y": 4, "c": 2}
ORDERS = (("x", "y", "z"), ("y", "z", "x"), ("z", "x", "y"))
ROWS = 768
WIDTH = 1024
HALF = 512
CAP = 12
GROUPS = 3
DEPTH = 4
DEVICES = 128
EDGE = 336
REST = ROWS - EDGE
PARTS = ((0, 256), (256, EDGE), (EDGE, EDGE + 256), (EDGE + 256, ROWS))
NT = (((1,), (1,)), ((), ()))
bf16, f32, i32 = jnp.bfloat16, jnp.float32, jnp.int32


def view(ref, *lead, **fixed):
    return ref.at[tuple(lead) + tuple(fixed.get(a, slice(None)) for a in AXES)]


def iota(shape, dim):
    return lax.broadcasted_iota(i32, shape, dim)


def dot(a, b, dims=(((1,), (0,)), ((), ())), exact=False):
    precision = lax.Precision.HIGHEST if exact else None
    return lax.dot_general(a, b, dims, precision=precision, preferred_element_type=f32)


def kernel(
    embed_hbm, target_hbm, rank_hbm, best_ref,
    target_ref, rank_ref, embed, scale, picks, unit, sent0, sent1, sent2, sent3, meta0, meta1, meta2, meta3, flat,
    slots, chosen, partly, own, from_prev, from_next, with_prev, with_next, returned, answer,
    load_sem, index_sem, sem1, sem2, sem3, out_sem, msem1, msem2, msem3, mout_sem,
    halo_sem, halo_out, last_sem, last_out, back_sem, back_out,
):
    grp, sub = lax.axis_index("grp"), lax.axis_index("sub")
    me = {"x": grp // 4, "z": lax.rem(grp, 4), "y": sub // 2, "c": lax.rem(sub, 2)}

    def device(**other):
        at = {**me, **other}
        return (at["x"] * 4 + at["z"], at["y"] * 2 + at["c"])

    def around(axis, by):
        return lax.rem(me[axis] + by, 4)

    def remote(src, dst, send_sem, recv_sem, to):
        pltpu.make_async_remote_copy(
            src_ref=src, dst_ref=dst, send_sem=send_sem, recv_sem=recv_sem,
            device_id=to, device_id_type=MESH,
        ).start()

    def landed(ref, sem):
        pltpu.make_async_copy(ref, ref, sem).wait()

    indices = [
        pltpu.make_async_copy(target_hbm, target_ref, index_sem.at[0]),
        pltpu.make_async_copy(rank_hbm, rank_ref, index_sem.at[1]),
    ]
    for load in indices:
        load.start()
    loads = []
    for i in range(3):
        part = pl.ds(i * 256, 256)
        loads.append(pltpu.make_async_copy(embed_hbm.at[part], embed.at[part], load_sem.at[i]))
        loads[-1].start()

    barrier = pltpu.get_barrier_semaphore()
    partners = [device(**{a: around(a, d)}) for a in "xyz" for d in (1, 2, 3)]
    partners += [device(**{a: around(a, d), "c": 1 - me["c"]}) for a in "xyz" for d in (1, 2, 3)]
    partners += [device(c=1 - me["c"])]
    for to in partners:
        pl.semaphore_signal(barrier, inc=1, device_id=to, device_id_type=MESH)

    chosen[:, 0:ROWS] = (iota((ROWS, ROWS), 0) < iota((ROWS, ROWS), 1)).astype(f32).astype(bf16)

    for load in indices:
        load.wait()
    target = target_ref[...].reshape(1, ROWS).astype(f32)
    rank = rank_ref[...].reshape(1, ROWS).astype(f32)
    owner = jnp.floor((target + 0.5) * (1.0 / ROWS))
    row = target - owner * ROWS
    owns = (owner == iota((DEVICES, ROWS), 0).astype(f32)).astype(f32)
    count = dot(owns.astype(bf16), chosen[:, 0:ROWS])
    within = jnp.sum(owns * count, axis=0, keepdims=True)
    code = owner * CAP + within
    def pick(g):
        k = iota((DEVICES * DEPTH, ROWS), 0)
        wanted = 3 * k - 2 * (k & 3) + DEPTH * g
        picks[g] = (code.astype(i32) == wanted).astype(f32).astype(bf16)

    pick(1)
    for i in range(3):
        loads[i].wait()

        for j in range(8):
            part = slice(i * 256 + j * 32, i * 256 + j * 32 + 32)
            e = embed[part, :]
            squares = jnp.sum(e * e, axis=1, keepdims=True)
            scale[part, :] = jnp.broadcast_to(lax.rsqrt(squares + 1e-06), (32, 128))
            unit[part, 0:HALF] = (e[:, 0:HALF] * jnp.tile(scale[part, :], (1, 4))).astype(bf16)

    def meta_first():
        lane_slot = iota((DEVICES, ROWS), 0).astype(f32)
        spread = jnp.where(within == lane_slot, row + 1.0, 0.0) + jnp.where(
            within + 16.0 == lane_slot, rank, 0.0
        )
        flat[...] = dot(owns, spread, NT, exact=True)
        for x in range(4):
            for z in range(4):
                for y in range(4):
                    for c in range(2):
                        at = ((x * 4 + z) * 4 + y) * 2 + c
                        meta0[x, z, y, c] = flat[at : at + 1, :]
        for d in (1, 3, 2):
            t = around("x", d)
            remote(view(meta0, x=t), view(meta1, x=me["x"]), mout_sem.at[0], msem1, device(x=t))
        pltpu.make_async_copy(view(meta0, x=me["x"]), view(meta1, x=me["x"]), msem1).start()

    def meta_second():
        landed(meta1, msem1)
        for d in (1, 3, 2):
            t = around("z", d)
            remote(view(meta1, z=t), view(meta2, z=me["z"]), mout_sem.at[1], msem2, device(z=t))
        pltpu.make_async_copy(view(meta1, z=me["z"]), view(meta2, z=me["z"]), msem2).start()

    def meta_third():
        landed(meta2, msem2)
        for d in (1, 3, 2, 0):
            t = around("y", d)
            for c in (me["c"], 1 - me["c"]):
                if d == 0 and c is me["c"]:
                    continue
                remote(
                    view(meta2, y=t, c=c), view(meta3, y=me["y"], c=me["c"]),
                    mout_sem.at[2], msem3, device(y=t, c=c),
                )
        here = {"y": me["y"], "c": me["c"]}
        pltpu.make_async_copy(view(meta2, **here), view(meta3, **here), msem3).start()

    def pack(h, g):
        q = dot(picks[g], unit[:, h * HALF : (h + 1) * HALF]).reshape(64, 8, HALF)
        r = pltpu.roll(q, 4, 1)
        low = iota((64, 8, 128), 1) < 4
        qs = [q[:, :, 128 * j : 128 * j + 128] for j in range(4)]
        rs = [r[:, :, 128 * j : 128 * j + 128] for j in range(4)]
        even = jnp.concatenate([jnp.where(low, qs[0], rs[1]), jnp.where(low, qs[2], rs[3])], axis=1)
        odd = jnp.concatenate([jnp.where(low, rs[0], qs[1]), jnp.where(low, rs[2], qs[3])], axis=1)
        sent0[h, g, :, :, :, 0] = even.astype(bf16).reshape(4, 4, 4, 16, 128)
        sent0[h, g, :, :, :, 1] = odd.astype(bf16).reshape(4, 4, 4, 16, 128)

    def first(h, g):
        a = ORDERS[g][0]
        for d in (1, 3, 2):
            t = around(a, d)
            remote(
                view(sent0, h, g, **{a: t}), view(sent1, h, g, **{a: me[a]}),
                out_sem.at[h, g, 0], sem1.at[h, g, me[a]], device(**{a: t}),
            )
        here = {a: me[a]}
        pltpu.make_async_copy(
            view(sent0, h, g, **here), view(sent1, h, g, **here), sem1.at[h, g, me[a]]
        ).start()

    def second(h, g, d0):
        a, b, _ = ORDERS[g]
        s = around(a, d0)
        landed(view(sent1, h, g, **{a: s}), sem1.at[h, g, s])
        for d in (1, 3, 2):
            t = around(b, d)
            remote(
                view(sent1, h, g, **{a: s, b: t}), view(sent2, h, g, **{a: s, b: me[b]}),
                out_sem.at[h, g, 1], sem2.at[h, g, me[b]], device(**{b: t}),
            )
        here = {a: s, b: me[b]}
        pltpu.make_async_copy(
            view(sent1, h, g, **here), view(sent2, h, g, **here), sem2.at[h, g, me[b]]
        ).start()

    def third(h, g, d0):
        _, b, e = ORDERS[g]
        s = around(b, d0)
        landed(view(sent2, h, g, **{b: s}), sem2.at[h, g, s])
        for d in (1, 3, 2, 0):
            t = around(e, d)
            for c in (me["c"], 1 - me["c"]):
                if d == 0 and c is me["c"]:
                    continue
                remote(
                    view(sent2, h, g, **{b: s, e: t, "c": c}),
                    view(sent3, h, g, **{b: s, e: me[e], "c": me["c"]}),
                    out_sem.at[h, g, 2], sem3.at[h, g], device(**{e: t, "c": c}),
                )
        here = {b: s, e: me[e], "c": me["c"]}
        pltpu.make_async_copy(
            view(sent2, h, g, **here), view(sent3, h, g, **here), sem3.at[h, g]
        ).start()

    def unpack(h, g):
        landed(sent3.at[h, g], sem3.at[h, g])
        even = sent3[h, g, :, :, :, 0].reshape(64, 16, 128).astype(f32)
        odd = sent3[h, g, :, :, :, 1].reshape(64, 16, 128).astype(f32)
        low = iota((64, 8, 128), 1) < 4
        rows = pl.ds(pl.multiple_of(g * 512, 512), 512)
        for j in range(2):
            a, b = even[:, 8 * j : 8 * j + 8], odd[:, 8 * j : 8 * j + 8]
            p = jnp.where(low, a, pltpu.roll(b, 4, 1)).reshape(512, 128)
            q = jnp.where(low, pltpu.roll(a, 4, 1), b).reshape(512, 128)
            slots[h, rows, 256 * j : 256 * j + 128] = p.astype(bf16)
            slots[h, rows, 256 * j + 128 : 256 * j + 256] = q.astype(bf16)

    later = (grp, lax.rem(sub + 1, 8))
    sooner = (grp, lax.rem(sub + 7, 8))

    def halo_sooner(h):
        remote(
            own.at[h, pl.ds(0, EDGE)], from_next.at[h],
            halo_out.at[1], halo_sem.at[1], sooner,
        )

    def halo_later(h):
        remote(
            own.at[h, pl.ds(EDGE, REST)], from_prev.at[h],
            halo_out.at[0], halo_sem.at[0], later,
        )

    def gather():
        own[0, 0:EDGE, :] = dot(chosen[0:EDGE, :], slots[0]).astype(bf16)
        halo_sooner(0)
        own[0, EDGE:ROWS, :] = dot(chosen[EDGE:ROWS, :], slots[0]).astype(bf16)
        halo_later(0)

    def gather_most():
        partly[...] = dot(chosen[:, 0:1024], slots[1, 0:1024])

    def gather_rest():
        for i, (lo, hi) in enumerate(PARTS):
            rest = dot(chosen[lo:hi, 1024:1536], slots[1, 1024:1536])
            own[1, lo:hi, :] = (partly[lo:hi, :] + rest).astype(bf16)
            if hi <= EDGE:
                there, to = from_next.at[1, pl.ds(lo, hi - lo)], sooner
            else:
                there, to = from_prev.at[1, pl.ds(lo - EDGE, hi - lo)], later
            remote(own.at[1, pl.ds(lo, hi - lo)], there, last_out.at[i], last_sem.at[i], to)

    def choose():
        landed(meta3, msem3)
        for x in range(4):
            for z in range(4):
                for y in range(4):
                    for c in range(2):
                        at = ((x * 4 + z) * 4 + y) * 2 + c
                        flat[at : at + 1, :] = meta3[x, z, y, c]
        got = flat[...]
        l, k = iota((128, 768), 0), iota((128, 768), 1)
        g, kind = (k // 128) % 3, k // 384
        expand = (l == kind * 16 + g * DEPTH + (k & 3)).astype(f32)
        wide = dot(got, expand, exact=True)
        mine = (iota((32, 128), 1) >> 2) == iota((32, 128), 0)

        def lanes(first):
            pieces = []
            for g in range(GROUPS):
                for j in range(4):
                    v = wide[32 * j : 32 * j + 32, first + 128 * g : first + 128 * g + 128]
                    pieces.append(jnp.sum(jnp.where(mine, v, 0.0), axis=0, keepdims=True))
            return jnp.concatenate(pieces, axis=1)

        place, its_rank = lanes(0), lanes(384)

        def build(j, _):
            part = pl.ds(pl.multiple_of(j * 64, 64), 64)
            r = (iota((64, 1536), 0) + j * 64 + 1).astype(f32)
            chosen[part, :] = (place == r).astype(f32).astype(bf16)
            return 0

        lax.fori_loop(0, 12, build, 0)
        high = jnp.floor(its_rank * (1.0 / 256.0))
        which = iota((16, 1536), 0)
        both = jnp.where(which == 0, high, jnp.where(which == 1, its_rank - 256.0 * high, 0.0))
        ranks = dot(both.astype(bf16), chosen[...], NT)
        rank_of = ranks[0:1] * 256.0 + ranks[1:2]
        return iota((1, ROWS), 1) - rank_of.astype(i32), rank_of[:, ROWS - 1 : ROWS].astype(i32)

    everyone = range(GROUPS)

    def repeat(step):
        def once(g, _):
            step(g)
            return 0

        lax.fori_loop(0, GROUPS, once, 0)

    pack(0, 1)
    pl.semaphore_wait(barrier, len(partners))
    first(0, 1)
    second(0, 1, 0)
    pick(0)
    pack(0, 0)
    first(0, 0)
    second(0, 0, 0)
    pick(2)
    pack(0, 2)
    first(0, 2)
    second(0, 2, 0)
    meta_first()

    def other_half(i, _):
        part = pl.ds(pl.multiple_of(i * 64, 64), 64)
        e = embed[part, HALF:WIDTH]
        unit[part, HALF:WIDTH] = (e * jnp.tile(scale[part, :], (1, 4))).astype(bf16)
        return 0

    lax.fori_loop(0, 12, other_half, 0)
    pack(1, 1)
    first(1, 1)
    for d in (1, 3, 2):
        for g in everyone:
            second(0, g, d)
    pack(1, 0)
    first(1, 0)
    second(1, 0, 0)
    pack(1, 2)
    first(1, 2)
    second(1, 1, 0)
    second(1, 2, 0)
    meta_second()
    for d in (0, 1, 3, 2):
        for g in (2, 0, 1):
            third(0, g, d)
    meta_third()
    for d in (1, 3, 2):
        for g in everyone:
            second(1, g, d)
    for g in (2, 0, 1):
        third(1, g, 0)
    begin, last_rank = choose()
    for d in (1, 3):
        for g in (2, 0, 1):
            third(1, g, d)
    repeat(lambda g: unpack(0, g))
    for g in (2, 0, 1):
        third(1, g, 2)
    gather()
    unpack(1, 0)
    unpack(1, 1)
    gather_most()
    unpack(1, 2)
    gather_rest()

    landed(from_next.at[0], halo_sem.at[1])
    with_next[...] = dot(own[0], from_next[0], NT)
    landed(from_prev.at[0], halo_sem.at[0])
    with_prev[...] = dot(from_prev[0], own[0], NT)

    here = []
    for j in range(3):
        n = 256 * (j + 1)
        p = slice(256 * j, n)
        s = dot(own[0, 0:n], own[0, p], NT) + dot(own[1, 0:n], own[1, p], NT)
        q, at = iota((n, 256), 0), iota((n, 256), 1) + 256 * j
        s = jnp.where((q >= begin[:, p]) & (q < at), s, -1.0)
        here.append(jnp.max(s, axis=0, keepdims=True))
    best = jnp.concatenate(here, axis=1)

    for h in range(2):
        for g in range(GROUPS):
            for phase in range(2):
                landed(sent0.at[h, g, pl.ds(0, 3)], out_sem.at[h, g, phase])
            landed(unit.at[pl.ds(0, 224)], out_sem.at[h, g, 2])
    landed(meta0.at[pl.ds(0, 3)], mout_sem.at[0])
    landed(meta0.at[pl.ds(0, 3)], mout_sem.at[1])
    landed(flat.at[pl.ds(0, 112)], mout_sem.at[2])

    for i, (lo, hi) in enumerate(PARTS[:2]):
        landed(from_next.at[1, pl.ds(lo, hi - lo)], last_sem.at[i])
        s = with_next[:, lo:hi] + dot(own[1], from_next[1, lo:hi], NT)
        s = jnp.where(iota((ROWS, hi - lo), 0) >= ROWS - 1 - last_rank, s, -1.0)
        answer[:, lo:hi] = jnp.max(s, axis=0, keepdims=True)
    remote(answer, returned, back_out, back_sem, later)

    for i, (lo, hi) in enumerate(PARTS[2:]):
        lo, hi = lo - EDGE, hi - EDGE
        landed(from_prev.at[1, pl.ds(lo, hi - lo)], last_sem.at[2 + i])
        s = with_prev[lo:hi, :] + dot(from_prev[1, lo:hi], own[1], NT)
        s = jnp.where(iota((hi - lo, ROWS), 0) + (lo - REST) >= begin, s, -1.0)
        best = jnp.maximum(best, jnp.max(s, axis=0, keepdims=True))
    landed(from_prev.at[0], halo_out.at[0])
    landed(from_next.at[0], halo_out.at[1])
    for i, (lo, hi) in enumerate(PARTS):
        landed(own.at[1, pl.ds(lo, hi - lo)], last_out.at[i])
    landed(returned, back_sem)
    back = jnp.concatenate([returned[...], jnp.full((1, ROWS - EDGE), -1.0, f32)], axis=1)
    best = jnp.maximum(best, jnp.where(begin < 0, back, -1.0))
    best_ref[...] = best.reshape(ROWS)
    landed(returned, back_out)


def per_device(embed, cluster, rank, target):
    blocks = (2, GROUPS, 4, 4, 4, 2, 16, 128)
    meta = (4, 4, 4, 2, 1, 128)
    dma = pltpu.SemaphoreType.DMA
    best = pl.pallas_call(
        kernel,
        out_shape=pltpu.VMEM((ROWS,), f32),
        in_specs=[
            pl.BlockSpec(memory_space=pl.ANY),
            pl.BlockSpec(memory_space=pl.ANY),
            pl.BlockSpec(memory_space=pl.ANY),
        ],
        out_specs=pl.BlockSpec(memory_space=pltpu.VMEM),
        scratch_shapes=[
            pltpu.VMEM((ROWS,), i32),
            pltpu.VMEM((ROWS,), i32),
            pltpu.VMEM((ROWS, WIDTH), f32),
            pltpu.VMEM((ROWS, 128), f32),
            pltpu.VMEM((GROUPS, DEVICES * DEPTH, ROWS), bf16),
            pltpu.VMEM((ROWS, WIDTH), bf16),
            *[pltpu.VMEM(blocks, bf16)] * 4,
            *[pltpu.VMEM(meta, f32)] * 4,
            pltpu.VMEM((DEVICES, 128), f32),
            pltpu.VMEM((2, GROUPS * 512, HALF), bf16),
            pltpu.VMEM((ROWS, GROUPS * 512), bf16),
            pltpu.VMEM((ROWS, HALF), f32),
            pltpu.VMEM((2, ROWS, HALF), bf16),
            pltpu.VMEM((2, REST, HALF), bf16),
            pltpu.VMEM((2, EDGE, HALF), bf16),
            pltpu.VMEM((REST, ROWS), f32),
            pltpu.VMEM((ROWS, EDGE), f32),
            pltpu.VMEM((1, EDGE), f32),
            pltpu.VMEM((1, EDGE), f32),
            dma((3,)),
            dma((2,)),
            dma((2, GROUPS, 4)),
            dma((2, GROUPS, 4)),
            dma((2, GROUPS)),
            dma((2, GROUPS, 3)),
            dma,
            dma,
            dma,
            dma((3,)),
            dma((2,)),
            dma((2,)),
            dma((4,)),
            dma((4,)),
            dma,
            dma,
        ],
        compiler_params=pltpu.CompilerParams(
            collective_id=0, has_side_effects=True, vmem_limit_bytes=56 * 2**20
        ),
        cost_estimate=pl.CostEstimate(flops=12 * 10**9, bytes_accessed=3 * 2**20, transcendentals=768),
    )(embed, target, rank)
    return best


def solution(mesh):
    in_specs = (P(("grp", "sub"), None), P(("grp", "sub")), P(("grp", "sub")), P(("grp", "sub")))
    out_specs = P(("grp", "sub"))
    return jax.shard_map(
        per_device, mesh=mesh, in_specs=in_specs, out_specs=out_specs, check_vma=False
    )
```

```python
import functools

import jax
import jax.numpy as jnp
from jax import lax
from jax.experimental import pallas as pl
from jax.experimental.pallas import tpu as pltpu
from jax.sharding import PartitionSpec as P

MESH = pl.DeviceIdType.MESH
AXES = ("x", "z", "y", "c")
SIZE = {"x": 4, "z": 4, "y": 4, "c": 2}
ORDERS = (("x", "y", "z"), ("y", "z", "x"), ("z", "x", "y"))
ROWS = 768
WIDTH = 1024
HALF = 512
CAP = 12
GROUPS = 3
DEPTH = 4
DEVICES = 128
EDGE = 320
REST = ROWS - EDGE
PARTS = ((0, 256), (256, EDGE), (EDGE, EDGE + 256), (EDGE + 256, ROWS))
NT = (((1,), (1,)), ((), ()))
bf16, f32, i32 = jnp.bfloat16, jnp.float32, jnp.int32


def view(ref, *lead, **fixed):
    return ref.at[tuple(lead) + tuple(fixed.get(a, slice(None)) for a in AXES)]


def iota(shape, dim):
    return lax.broadcasted_iota(i32, shape, dim)


def dot(a, b, dims=(((1,), (0,)), ((), ())), exact=False):
    precision = lax.Precision.HIGHEST if exact else None
    return lax.dot_general(a, b, dims, precision=precision, preferred_element_type=f32)


def kernel(
    embed_hbm, target_hbm, rank_hbm, best_ref,
    target_ref, rank_ref, embed, scale, picks, unit, sent0, sent1, sent2, sent3, meta0, meta1, meta2, meta3, flat,
    slots, chosen, partly, own, from_prev, from_next, with_prev, with_next, returned, answer,
    load_sem, index_sem, sem1, sem2, sem3, out_sem, msem1, msem2, msem3, mout_sem,
    halo_sem, halo_out, last_sem, last_out, back_sem, back_out,
):
    grp, sub = lax.axis_index("grp"), lax.axis_index("sub")
    me = {"x": grp // 4, "z": lax.rem(grp, 4), "y": sub // 2, "c": lax.rem(sub, 2)}

    def device(**other):
        at = {**me, **other}
        return (at["x"] * 4 + at["z"], at["y"] * 2 + at["c"])

    def around(axis, by):
        return lax.rem(me[axis] + by, 4)

    def remote(src, dst, send_sem, recv_sem, to):
        pltpu.make_async_remote_copy(
            src_ref=src, dst_ref=dst, send_sem=send_sem, recv_sem=recv_sem,
            device_id=to, device_id_type=MESH,
        ).start()

    def landed(ref, sem):
        pltpu.make_async_copy(ref, ref, sem).wait()

    indices = [
        pltpu.make_async_copy(target_hbm, target_ref, index_sem.at[0]),
        pltpu.make_async_copy(rank_hbm, rank_ref, index_sem.at[1]),
    ]
    for load in indices:
        load.start()
    loads = []
    for i in range(3):
        part = pl.ds(i * 256, 256)
        loads.append(pltpu.make_async_copy(embed_hbm.at[part], embed.at[part], load_sem.at[i]))
        loads[-1].start()

    barrier = pltpu.get_barrier_semaphore()
    partners = [device(**{a: around(a, d)}) for a in "xyz" for d in (1, 2, 3)]
    partners += [device(**{a: around(a, d), "c": 1 - me["c"]}) for a in "xyz" for d in (1, 2, 3)]
    partners += [device(c=1 - me["c"])]
    for to in partners:
        pl.semaphore_signal(barrier, inc=1, device_id=to, device_id_type=MESH)

    chosen[:, 0:ROWS] = (iota((ROWS, ROWS), 0) < iota((ROWS, ROWS), 1)).astype(f32).astype(bf16)

    for load in indices:
        load.wait()
    target = target_ref[...].reshape(1, ROWS).astype(f32)
    rank = rank_ref[...].reshape(1, ROWS).astype(f32)
    owner = jnp.floor((target + 0.5) * (1.0 / ROWS))
    row = target - owner * ROWS
    owns = (owner == iota((DEVICES, ROWS), 0).astype(f32)).astype(f32)
    count = dot(owns.astype(bf16), chosen[:, 0:ROWS])
    within = jnp.sum(owns * count, axis=0, keepdims=True)
    code = owner * CAP + within
    def pick(g):
        k = iota((DEVICES * DEPTH, ROWS), 0)
        wanted = 3 * k - 2 * (k & 3) + DEPTH * g
        picks[g] = (code.astype(i32) == wanted).astype(f32).astype(bf16)

    pick(1)
    for load in loads:
        load.wait()
    early = jnp.zeros((DEVICES * DEPTH, HALF), f32)
    for i in range(3):
        half = []
        for j in range(8):
            part = slice(i * 256 + j * 32, i * 256 + j * 32 + 32)
            e = embed[part, :]
            squares = jnp.sum(e * e, axis=1, keepdims=True)
            scale[part, :] = jnp.broadcast_to(lax.rsqrt(squares + 1e-06), (32, 128))
            half.append((e[:, 0:HALF] * lax.rsqrt(squares + 1e-06)).astype(bf16))
            unit[part, 0:HALF] = half[-1]
        early += dot(picks[1, :, i * 256 : i * 256 + 256], jnp.concatenate(half, axis=0))

    def meta_first():
        lane_slot = iota((DEVICES, ROWS), 0).astype(f32)
        spread = jnp.where(within == lane_slot, row + 1.0, 0.0) + jnp.where(
            within + 16.0 == lane_slot, rank, 0.0
        )
        flat[...] = dot(owns, spread, NT, exact=True)
        for x in range(4):
            for z in range(4):
                for y in range(4):
                    for c in range(2):
                        at = ((x * 4 + z) * 4 + y) * 2 + c
                        meta0[x, z, y, c] = flat[at : at + 1, :]
        for d in (1, 3, 2):
            t = around("x", d)
            remote(view(meta0, x=t), view(meta1, x=me["x"]), mout_sem.at[0], msem1, device(x=t))
        pltpu.make_async_copy(view(meta0, x=me["x"]), view(meta1, x=me["x"]), msem1).start()

    def meta_second():
        landed(meta1, msem1)
        for d in (1, 3, 2):
            t = around("z", d)
            remote(view(meta1, z=t), view(meta2, z=me["z"]), mout_sem.at[1], msem2, device(z=t))
        pltpu.make_async_copy(view(meta1, z=me["z"]), view(meta2, z=me["z"]), msem2).start()

    def meta_third():
        landed(meta2, msem2)
        for d in (1, 3, 2, 0):
            t = around("y", d)
            for c in (me["c"], 1 - me["c"]):
                if d == 0 and c is me["c"]:
                    continue
                remote(
                    view(meta2, y=t, c=c), view(meta3, y=me["y"], c=me["c"]),
                    mout_sem.at[2], msem3, device(y=t, c=c),
                )
        here = {"y": me["y"], "c": me["c"]}
        pltpu.make_async_copy(view(meta2, **here), view(meta3, **here), msem3).start()

    def pack(h, g):
        finish(h, g, dot(picks[g], unit[:, h * HALF : (h + 1) * HALF]))

    def finish(h, g, q):
        q = q.reshape(64, 8, HALF)
        r = pltpu.roll(q, 4, 1)
        low = iota((64, 8, 128), 1) < 4
        qs = [q[:, :, 128 * j : 128 * j + 128] for j in range(4)]
        rs = [r[:, :, 128 * j : 128 * j + 128] for j in range(4)]
        even = jnp.concatenate([jnp.where(low, qs[0], rs[1]), jnp.where(low, qs[2], rs[3])], axis=1)
        odd = jnp.concatenate([jnp.where(low, rs[0], qs[1]), jnp.where(low, rs[2], qs[3])], axis=1)
        sent0[h, g, :, :, :, 0] = even.astype(bf16).reshape(4, 4, 4, 16, 128)
        sent0[h, g, :, :, :, 1] = odd.astype(bf16).reshape(4, 4, 4, 16, 128)

    def first(h, g):
        a = ORDERS[g][0]
        for d in (1, 3, 2):
            t = around(a, d)
            remote(
                view(sent0, h, g, **{a: t}), view(sent1, h, g, **{a: me[a]}),
                out_sem.at[h, g, 0], sem1.at[h, g, me[a]], device(**{a: t}),
            )
        here = {a: me[a]}
        pltpu.make_async_copy(
            view(sent0, h, g, **here), view(sent1, h, g, **here), sem1.at[h, g, me[a]]
        ).start()

    def second(h, g, d0):
        a, b, _ = ORDERS[g]
        s = around(a, d0)
        landed(view(sent1, h, g, **{a: s}), sem1.at[h, g, s])
        for d in (1, 3, 2):
            t = around(b, d)
            remote(
                view(sent1, h, g, **{a: s, b: t}), view(sent2, h, g, **{a: s, b: me[b]}),
                out_sem.at[h, g, 1], sem2.at[h, g, me[b]], device(**{b: t}),
            )
        here = {a: s, b: me[b]}
        pltpu.make_async_copy(
            view(sent1, h, g, **here), view(sent2, h, g, **here), sem2.at[h, g, me[b]]
        ).start()

    def third(h, g, d0):
        _, b, e = ORDERS[g]
        s = around(b, d0)
        landed(view(sent2, h, g, **{b: s}), sem2.at[h, g, s])
        for d in (1, 3, 2, 0):
            t = around(e, d)
            for c in (me["c"], 1 - me["c"]):
                if d == 0 and c is me["c"]:
                    continue
                remote(
                    view(sent2, h, g, **{b: s, e: t, "c": c}),
                    view(sent3, h, g, **{b: s, e: me[e], "c": me["c"]}),
                    out_sem.at[h, g, 2], sem3.at[h, g], device(**{e: t, "c": c}),
                )
        here = {b: s, e: me[e], "c": me["c"]}
        pltpu.make_async_copy(
            view(sent2, h, g, **here), view(sent3, h, g, **here), sem3.at[h, g]
        ).start()

    def unpack(h, g):
        landed(sent3.at[h, g], sem3.at[h, g])
        even = sent3[h, g, :, :, :, 0].reshape(64, 16, 128).astype(f32)
        odd = sent3[h, g, :, :, :, 1].reshape(64, 16, 128).astype(f32)
        low = iota((64, 8, 128), 1) < 4
        rows = pl.ds(pl.multiple_of(g * 512, 512), 512)
        for j in range(2):
            a, b = even[:, 8 * j : 8 * j + 8], odd[:, 8 * j : 8 * j + 8]
            p = jnp.where(low, a, pltpu.roll(b, 4, 1)).reshape(512, 128)
            q = jnp.where(low, pltpu.roll(a, 4, 1), b).reshape(512, 128)
            slots[h, rows, 256 * j : 256 * j + 128] = p.astype(bf16)
            slots[h, rows, 256 * j + 128 : 256 * j + 256] = q.astype(bf16)

    later = (grp, lax.rem(sub + 1, 8))
    sooner = (grp, lax.rem(sub + 7, 8))

    def halo_sooner(h):
        remote(
            own.at[h, pl.ds(0, EDGE)], from_next.at[h],
            halo_out.at[1], halo_sem.at[1], sooner,
        )

    def halo_later(h):
        remote(
            own.at[h, pl.ds(EDGE, REST)], from_prev.at[h],
            halo_out.at[0], halo_sem.at[0], later,
        )

    def gather():
        own[0, 0:EDGE, :] = dot(chosen[0:EDGE, :], slots[0]).astype(bf16)
        halo_sooner(0)
        own[0, EDGE:ROWS, :] = dot(chosen[EDGE:ROWS, :], slots[0]).astype(bf16)
        halo_later(0)

    def gather_most():
        partly[...] = dot(chosen[:, 0:1024], slots[1, 0:1024])

    def gather_rest():
        for i in (0, 2, 1, 3):
            lo, hi = PARTS[i]
            rest = dot(chosen[lo:hi, 1024:1536], slots[1, 1024:1536])
            own[1, lo:hi, :] = (partly[lo:hi, :] + rest).astype(bf16)
            if hi <= EDGE:
                there, to = from_next.at[1, pl.ds(lo, hi - lo)], sooner
            else:
                there, to = from_prev.at[1, pl.ds(lo - EDGE, hi - lo)], later
            remote(own.at[1, pl.ds(lo, hi - lo)], there, last_out.at[i], last_sem.at[i], to)

    def choose():
        landed(meta3, msem3)
        for x in range(4):
            for z in range(4):
                for y in range(4):
                    for c in range(2):
                        at = ((x * 4 + z) * 4 + y) * 2 + c
                        flat[at : at + 1, :] = meta3[x, z, y, c]
        got = flat[...]
        l, k = iota((128, 768), 0), iota((128, 768), 1)
        g, kind = (k // 128) % 3, k // 384
        expand = (l == kind * 16 + g * DEPTH + (k & 3)).astype(f32)
        wide = dot(got, expand, exact=True)
        mine = (iota((32, 128), 1) >> 2) == iota((32, 128), 0)

        def lanes(first):
            pieces = []
            for g in range(GROUPS):
                for j in range(4):
                    v = wide[32 * j : 32 * j + 32, first + 128 * g : first + 128 * g + 128]
                    pieces.append(jnp.sum(jnp.where(mine, v, 0.0), axis=0, keepdims=True))
            return jnp.concatenate(pieces, axis=1)

        place, its_rank = lanes(0), lanes(384)

        def build(j, _):
            part = pl.ds(pl.multiple_of(j * 64, 64), 64)
            r = (iota((64, 1536), 0) + j * 64 + 1).astype(f32)
            chosen[part, :] = (place == r).astype(f32).astype(bf16)
            return 0

        lax.fori_loop(0, 12, build, 0)
        high = jnp.floor(its_rank * (1.0 / 256.0))
        which = iota((16, 1536), 0)
        both = jnp.where(which == 0, high, jnp.where(which == 1, its_rank - 256.0 * high, 0.0))
        ranks = dot(both.astype(bf16), chosen[...], NT)
        rank_of = ranks[0:1] * 256.0 + ranks[1:2]
        return iota((1, ROWS), 1) - rank_of.astype(i32), rank_of[:, ROWS - 1 : ROWS].astype(i32)

    everyone = range(GROUPS)

    def repeat(step):
        def once(g, _):
            step(g)
            return 0

        lax.fori_loop(0, GROUPS, once, 0)

    finish(0, 1, early)
    pl.semaphore_wait(barrier, len(partners))
    first(0, 1)
    second(0, 1, 0)
    pick(0)
    pack(0, 0)
    first(0, 0)
    second(0, 0, 0)
    pick(2)
    pack(0, 2)
    first(0, 2)
    second(0, 2, 0)
    meta_first()

    def other_half(i, _):
        part = pl.ds(pl.multiple_of(i * 64, 64), 64)
        e = embed[part, HALF:WIDTH]
        unit[part, HALF:WIDTH] = (e * jnp.tile(scale[part, :], (1, 4))).astype(bf16)
        return 0

    lax.fori_loop(0, 12, other_half, 0)
    pack(1, 1)
    first(1, 1)
    for d in (1, 3, 2):
        for g in everyone:
            second(0, g, d)
    pack(1, 0)
    first(1, 0)
    second(1, 0, 0)
    pack(1, 2)
    first(1, 2)
    second(1, 1, 0)
    second(1, 2, 0)
    meta_second()
    for d in (0, 1, 3, 2):
        for g in (2, 0, 1):
            third(0, g, d)
    meta_third()
    for d in (1, 3, 2):
        for g in everyone:
            second(1, g, d)
    for g in (2, 0, 1):
        third(1, g, 0)
    begin, last_rank = choose()
    for d in (1, 3):
        for g in (2, 0, 1):
            third(1, g, d)
    repeat(lambda g: unpack(0, g))
    for g in (2, 0, 1):
        third(1, g, 2)
    gather()
    unpack(1, 0)
    unpack(1, 1)
    gather_most()
    unpack(1, 2)
    gather_rest()

    landed(from_next.at[0], halo_sem.at[1])
    with_next[...] = dot(own[0], from_next[0], NT)
    landed(from_prev.at[0], halo_sem.at[0])
    with_prev[...] = dot(from_prev[0], own[0], NT)

    here = []
    for j in range(3):
        n = 256 * (j + 1)
        p = slice(256 * j, n)
        s = dot(own[0, 0:n], own[0, p], NT) + dot(own[1, 0:n], own[1, p], NT)
        q, at = iota((n, 256), 0), iota((n, 256), 1) + 256 * j
        s = jnp.where((q >= begin[:, p]) & (q < at), s, -1.0)
        here.append(jnp.max(s, axis=0, keepdims=True))
    best = jnp.concatenate(here, axis=1)

    for h in range(2):
        for g in range(GROUPS):
            for phase in range(2):
                landed(sent0.at[h, g, pl.ds(0, 3)], out_sem.at[h, g, phase])
            landed(unit.at[pl.ds(0, 224)], out_sem.at[h, g, 2])
    landed(meta0.at[pl.ds(0, 3)], mout_sem.at[0])
    landed(meta0.at[pl.ds(0, 3)], mout_sem.at[1])
    landed(flat.at[pl.ds(0, 112)], mout_sem.at[2])

    for i, (lo, hi) in enumerate(PARTS[:2]):
        landed(from_next.at[1, pl.ds(lo, hi - lo)], last_sem.at[i])
        s = with_next[:, lo:hi] + dot(own[1], from_next[1, lo:hi], NT)
        s = jnp.where(iota((ROWS, hi - lo), 0) >= ROWS - 1 - last_rank, s, -1.0)
        answer[:, lo:hi] = jnp.max(s, axis=0, keepdims=True)
    remote(answer, returned, back_out, back_sem, later)

    for i, (lo, hi) in enumerate(PARTS[2:]):
        lo, hi = lo - EDGE, hi - EDGE
        landed(from_prev.at[1, pl.ds(lo, hi - lo)], last_sem.at[2 + i])
        s = with_prev[lo:hi, :] + dot(from_prev[1, lo:hi], own[1], NT)
        s = jnp.where(iota((hi - lo, ROWS), 0) + (lo - REST) >= begin, s, -1.0)
        best = jnp.maximum(best, jnp.max(s, axis=0, keepdims=True))
    landed(from_prev.at[0], halo_out.at[0])
    landed(from_next.at[0], halo_out.at[1])
    for i, (lo, hi) in enumerate(PARTS):
        landed(own.at[1, pl.ds(lo, hi - lo)], last_out.at[i])
    landed(returned, back_sem)
    back = jnp.concatenate([returned[...], jnp.full((1, ROWS - EDGE), -1.0, f32)], axis=1)
    best = jnp.maximum(best, jnp.where(begin < 0, back, -1.0))
    best_ref[...] = best.reshape(ROWS)
    landed(returned, back_out)


def per_device(embed, cluster, rank, target):
    blocks = (2, GROUPS, 4, 4, 4, 2, 16, 128)
    meta = (4, 4, 4, 2, 1, 128)
    dma = pltpu.SemaphoreType.DMA
    best = pl.pallas_call(
        kernel,
        out_shape=pltpu.VMEM((ROWS,), f32),
        in_specs=[
            pl.BlockSpec(memory_space=pl.ANY),
            pl.BlockSpec(memory_space=pl.ANY),
            pl.BlockSpec(memory_space=pl.ANY),
        ],
        out_specs=pl.BlockSpec(memory_space=pltpu.VMEM),
        scratch_shapes=[
            pltpu.VMEM((ROWS,), i32),
            pltpu.VMEM((ROWS,), i32),
            pltpu.VMEM((ROWS, WIDTH), f32),
            pltpu.VMEM((ROWS, 128), f32),
            pltpu.VMEM((GROUPS, DEVICES * DEPTH, ROWS), bf16),
            pltpu.VMEM((ROWS, WIDTH), bf16),
            *[pltpu.VMEM(blocks, bf16)] * 4,
            *[pltpu.VMEM(meta, f32)] * 4,
            pltpu.VMEM((DEVICES, 128), f32),
            pltpu.VMEM((2, GROUPS * 512, HALF), bf16),
            pltpu.VMEM((ROWS, GROUPS * 512), bf16),
            pltpu.VMEM((ROWS, HALF), f32),
            pltpu.VMEM((2, ROWS, HALF), bf16),
            pltpu.VMEM((2, REST, HALF), bf16),
            pltpu.VMEM((2, EDGE, HALF), bf16),
            pltpu.VMEM((REST, ROWS), f32),
            pltpu.VMEM((ROWS, EDGE), f32),
            pltpu.VMEM((1, EDGE), f32),
            pltpu.VMEM((1, EDGE), f32),
            dma((3,)),
            dma((2,)),
            dma((2, GROUPS, 4)),
            dma((2, GROUPS, 4)),
            dma((2, GROUPS)),
            dma((2, GROUPS, 3)),
            dma,
            dma,
            dma,
            dma((3,)),
            dma((2,)),
            dma((2,)),
            dma((4,)),
            dma((4,)),
            dma,
            dma,
        ],
        compiler_params=pltpu.CompilerParams(
            collective_id=0, has_side_effects=True, vmem_limit_bytes=56 * 2**20
        ),
        cost_estimate=pl.CostEstimate(flops=12 * 10**9, bytes_accessed=3 * 2**20, transcendentals=768),
    )(embed, target, rank)
    return best


def solution(mesh):
    in_specs = (P(("grp", "sub"), None), P(("grp", "sub")), P(("grp", "sub")), P(("grp", "sub")))
    out_specs = P(("grp", "sub"))
    return jax.shard_map(
        per_device, mesh=mesh, in_specs=in_specs, out_specs=out_specs, check_vma=False
    )
```

```python
import functools

import jax
import jax.numpy as jnp
from jax import lax
from jax.experimental import pallas as pl
from jax.experimental.pallas import tpu as pltpu
from jax.sharding import PartitionSpec as P

MESH = pl.DeviceIdType.MESH
AXES = ("x", "z", "y", "c")
SIZE = {"x": 4, "z": 4, "y": 4, "c": 2}
ORDERS = (("x", "y", "z"), ("y", "z", "x"), ("z", "x", "y"))
ROWS = 768
WIDTH = 1024
HALF = 512
CAP = 12
GROUPS = 3
DEPTH = 4
DEVICES = 128
EDGE = 320
REST = ROWS - EDGE
PARTS = ((0, 256), (256, EDGE), (EDGE, EDGE + 256), (EDGE + 256, ROWS))
NT = (((1,), (1,)), ((), ()))
bf16, f32, i32 = jnp.bfloat16, jnp.float32, jnp.int32


def view(ref, *lead, **fixed):
    return ref.at[tuple(lead) + tuple(fixed.get(a, slice(None)) for a in AXES)]


def iota(shape, dim):
    return lax.broadcasted_iota(i32, shape, dim)


def dot(a, b, dims=(((1,), (0,)), ((), ())), exact=False):
    precision = lax.Precision.HIGHEST if exact else None
    return lax.dot_general(a, b, dims, precision=precision, preferred_element_type=f32)


def kernel(
    embed_hbm, target_hbm, rank_hbm, best_ref,
    target_ref, rank_ref, embed, scale, picks, unit, sent0, sent1, sent2, sent3, meta0, meta1, meta2, meta3, flat,
    slots, chosen, partly, own, from_prev, from_next, with_prev, with_next, returned, answer,
    load_sem, index_sem, sem1, sem2, sem3, out_sem, msem1, msem2, msem3, mout_sem,
    halo_sem, halo_out, last_sem, last_out, back_sem, back_out,
):
    grp, sub = lax.axis_index("grp"), lax.axis_index("sub")
    me = {"x": grp // 4, "z": lax.rem(grp, 4), "y": sub // 2, "c": lax.rem(sub, 2)}

    def device(**other):
        at = {**me, **other}
        return (at["x"] * 4 + at["z"], at["y"] * 2 + at["c"])

    def around(axis, by):
        return lax.rem(me[axis] + by, 4)

    def remote(src, dst, send_sem, recv_sem, to):
        pltpu.make_async_remote_copy(
            src_ref=src, dst_ref=dst, send_sem=send_sem, recv_sem=recv_sem,
            device_id=to, device_id_type=MESH,
        ).start()

    def landed(ref, sem):
        pltpu.make_async_copy(ref, ref, sem).wait()

    indices = [
        pltpu.make_async_copy(target_hbm, target_ref, index_sem.at[0]),
        pltpu.make_async_copy(rank_hbm, rank_ref, index_sem.at[1]),
    ]
    for load in indices:
        load.start()
    loads = []
    for i in range(3):
        part = pl.ds(i * 256, 256)
        loads.append(pltpu.make_async_copy(embed_hbm.at[part], embed.at[part], load_sem.at[i]))
        loads[-1].start()

    barrier = pltpu.get_barrier_semaphore()
    partners = [device(**{a: around(a, d)}) for a in "xyz" for d in (1, 2, 3)]
    partners += [device(**{a: around(a, d), "c": 1 - me["c"]}) for a in "xyz" for d in (1, 2, 3)]
    partners += [device(c=1 - me["c"])]
    for to in partners:
        pl.semaphore_signal(barrier, inc=1, device_id=to, device_id_type=MESH)

    chosen[:, 0:ROWS] = (iota((ROWS, ROWS), 0) < iota((ROWS, ROWS), 1)).astype(f32).astype(bf16)

    for load in indices:
        load.wait()
    target = target_ref[...].reshape(1, ROWS).astype(f32)
    rank = rank_ref[...].reshape(1, ROWS).astype(f32)
    owner = jnp.floor((target + 0.5) * (1.0 / ROWS))
    row = target - owner * ROWS
    owns = (owner == iota((DEVICES, ROWS), 0).astype(f32)).astype(f32)
    count = dot(owns.astype(bf16), chosen[:, 0:ROWS])
    within = jnp.sum(owns * count, axis=0, keepdims=True)
    code = owner * CAP + within
    def pick(g):
        k = iota((DEVICES * DEPTH, ROWS), 0)
        wanted = 3 * k - 2 * (k & 3) + DEPTH * g
        picks[g] = (code.astype(i32) == wanted).astype(f32).astype(bf16)

    pick(1)
    for load in loads:
        load.wait()
    early = jnp.zeros((DEVICES * DEPTH, HALF), f32)
    for i in range(3):
        half = []
        for j in range(8):
            part = slice(i * 256 + j * 32, i * 256 + j * 32 + 32)
            e = embed[part, :]
            squares = jnp.sum(e * e, axis=1, keepdims=True)
            scale[part, :] = jnp.broadcast_to(lax.rsqrt(squares + 1e-06), (32, 128))
            half.append((e[:, 0:HALF] * lax.rsqrt(squares + 1e-06)).astype(bf16))
            unit[part, 0:HALF] = half[-1]
        early += dot(picks[1, :, i * 256 : i * 256 + 256], jnp.concatenate(half, axis=0))

    def meta_first():
        lane_slot = iota((DEVICES, ROWS), 0).astype(f32)
        spread = jnp.where(within == lane_slot, row + 1.0, 0.0) + jnp.where(
            within + 16.0 == lane_slot, rank, 0.0
        )
        flat[...] = dot(owns, spread, NT, exact=True)
        for x in range(4):
            for z in range(4):
                for y in range(4):
                    for c in range(2):
                        at = ((x * 4 + z) * 4 + y) * 2 + c
                        meta0[x, z, y, c] = flat[at : at + 1, :]
        for d in (1, 3, 2):
            t = around("x", d)
            remote(view(meta0, x=t), view(meta1, x=me["x"]), mout_sem.at[0], msem1, device(x=t))
        pltpu.make_async_copy(view(meta0, x=me["x"]), view(meta1, x=me["x"]), msem1).start()

    def meta_second():
        landed(meta1, msem1)
        for d in (1, 3, 2):
            t = around("z", d)
            remote(view(meta1, z=t), view(meta2, z=me["z"]), mout_sem.at[1], msem2, device(z=t))
        pltpu.make_async_copy(view(meta1, z=me["z"]), view(meta2, z=me["z"]), msem2).start()

    def meta_third():
        landed(meta2, msem2)
        for d in (1, 3, 2, 0):
            t = around("y", d)
            for c in (me["c"], 1 - me["c"]):
                if d == 0 and c is me["c"]:
                    continue
                remote(
                    view(meta2, y=t, c=c), view(meta3, y=me["y"], c=me["c"]),
                    mout_sem.at[2], msem3, device(y=t, c=c),
                )
        here = {"y": me["y"], "c": me["c"]}
        pltpu.make_async_copy(view(meta2, **here), view(meta3, **here), msem3).start()

    def pack(h, g):
        finish(h, g, dot(picks[g], unit[:, h * HALF : (h + 1) * HALF]))

    def finish(h, g, q):
        q = q.reshape(64, 8, HALF)
        r = pltpu.roll(q, 4, 1)
        low = iota((64, 8, 128), 1) < 4
        qs = [q[:, :, 128 * j : 128 * j + 128] for j in range(4)]
        rs = [r[:, :, 128 * j : 128 * j + 128] for j in range(4)]
        even = jnp.concatenate([jnp.where(low, qs[0], rs[1]), jnp.where(low, qs[2], rs[3])], axis=1)
        odd = jnp.concatenate([jnp.where(low, rs[0], qs[1]), jnp.where(low, rs[2], qs[3])], axis=1)
        sent0[h, g, :, :, :, 0] = even.astype(bf16).reshape(4, 4, 4, 16, 128)
        sent0[h, g, :, :, :, 1] = odd.astype(bf16).reshape(4, 4, 4, 16, 128)

    def first(h, g):
        a = ORDERS[g][0]
        for d in (1, 3, 2):
            t = around(a, d)
            remote(
                view(sent0, h, g, **{a: t}), view(sent1, h, g, **{a: me[a]}),
                out_sem.at[h, g, 0], sem1.at[h, g, me[a]], device(**{a: t}),
            )
        here = {a: me[a]}
        pltpu.make_async_copy(
            view(sent0, h, g, **here), view(sent1, h, g, **here), sem1.at[h, g, me[a]]
        ).start()

    def second(h, g, d0):
        a, b, _ = ORDERS[g]
        s = around(a, d0)
        landed(view(sent1, h, g, **{a: s}), sem1.at[h, g, s])
        for d in (1, 3, 2):
            t = around(b, d)
            remote(
                view(sent1, h, g, **{a: s, b: t}), view(sent2, h, g, **{a: s, b: me[b]}),
                out_sem.at[h, g, 1], sem2.at[h, g, me[b]], device(**{b: t}),
            )
        here = {a: s, b: me[b]}
        pltpu.make_async_copy(
            view(sent1, h, g, **here), view(sent2, h, g, **here), sem2.at[h, g, me[b]]
        ).start()

    def third(h, g, d0):
        _, b, e = ORDERS[g]
        s = around(b, d0)
        landed(view(sent2, h, g, **{b: s}), sem2.at[h, g, s])
        for d in (1, 3, 2, 0):
            t = around(e, d)
            for c in (me["c"], 1 - me["c"]):
                if d == 0 and c is me["c"]:
                    continue
                remote(
                    view(sent2, h, g, **{b: s, e: t, "c": c}),
                    view(sent3, h, g, **{b: s, e: me[e], "c": me["c"]}),
                    out_sem.at[h, g, 2], sem3.at[h, g], device(**{e: t, "c": c}),
                )
        here = {b: s, e: me[e], "c": me["c"]}
        pltpu.make_async_copy(
            view(sent2, h, g, **here), view(sent3, h, g, **here), sem3.at[h, g]
        ).start()

    def unpack(h, g):
        landed(sent3.at[h, g], sem3.at[h, g])
        even = sent3[h, g, :, :, :, 0].reshape(64, 16, 128).astype(f32)
        odd = sent3[h, g, :, :, :, 1].reshape(64, 16, 128).astype(f32)
        low = iota((64, 8, 128), 1) < 4
        rows = pl.ds(pl.multiple_of(g * 512, 512), 512)
        for j in range(2):
            a, b = even[:, 8 * j : 8 * j + 8], odd[:, 8 * j : 8 * j + 8]
            p = jnp.where(low, a, pltpu.roll(b, 4, 1)).reshape(512, 128)
            q = jnp.where(low, pltpu.roll(a, 4, 1), b).reshape(512, 128)
            slots[h, rows, 256 * j : 256 * j + 128] = p.astype(bf16)
            slots[h, rows, 256 * j + 128 : 256 * j + 256] = q.astype(bf16)

    later = (grp, lax.rem(sub + 1, 8))
    sooner = (grp, lax.rem(sub + 7, 8))

    def halo_sooner(h):
        remote(
            own.at[h, pl.ds(0, EDGE)], from_next.at[h],
            halo_out.at[1], halo_sem.at[1], sooner,
        )

    def halo_later(h):
        remote(
            own.at[h, pl.ds(EDGE, REST)], from_prev.at[h],
            halo_out.at[0], halo_sem.at[0], later,
        )

    def gather():
        own[0, 0:EDGE, :] = dot(chosen[0:EDGE, :], slots[0]).astype(bf16)
        halo_sooner(0)
        own[0, EDGE:ROWS, :] = dot(chosen[EDGE:ROWS, :], slots[0]).astype(bf16)
        halo_later(0)

    def gather_most():
        partly[...] = dot(chosen[:, 0:1024], slots[1, 0:1024])

    def gather_rest():
        for i in (0, 2, 1, 3):
            lo, hi = PARTS[i]
            rest = dot(chosen[lo:hi, 1024:1536], slots[1, 1024:1536])
            own[1, lo:hi, :] = (partly[lo:hi, :] + rest).astype(bf16)
            if hi <= EDGE:
                there, to = from_next.at[1, pl.ds(lo, hi - lo)], sooner
            else:
                there, to = from_prev.at[1, pl.ds(lo - EDGE, hi - lo)], later
            remote(own.at[1, pl.ds(lo, hi - lo)], there, last_out.at[i], last_sem.at[i], to)

    def choose():
        landed(meta3, msem3)
        for x in range(4):
            for z in range(4):
                for y in range(4):
                    for c in range(2):
                        at = ((x * 4 + z) * 4 + y) * 2 + c
                        flat[at : at + 1, :] = meta3[x, z, y, c]
        got = flat[...]
        l, k = iota((128, 768), 0), iota((128, 768), 1)
        g, kind = (k // 128) % 3, k // 384
        expand = (l == kind * 16 + g * DEPTH + (k & 3)).astype(f32)
        wide = dot(got, expand, exact=True)
        mine = (iota((32, 128), 1) >> 2) == iota((32, 128), 0)

        def lanes(first):
            pieces = []
            for g in range(GROUPS):
                for j in range(4):
                    v = wide[32 * j : 32 * j + 32, first + 128 * g : first + 128 * g + 128]
                    pieces.append(jnp.sum(jnp.where(mine, v, 0.0), axis=0, keepdims=True))
            return jnp.concatenate(pieces, axis=1)

        place, its_rank = lanes(0), lanes(384)

        def build(j, _):
            part = pl.ds(pl.multiple_of(j * 64, 64), 64)
            r = (iota((64, 1536), 0) + j * 64 + 1).astype(f32)
            chosen[part, :] = (place == r).astype(f32).astype(bf16)
            return 0

        lax.fori_loop(0, 12, build, 0)
        high = jnp.floor(its_rank * (1.0 / 256.0))
        which = iota((16, 1536), 0)
        both = jnp.where(which == 0, high, jnp.where(which == 1, its_rank - 256.0 * high, 0.0))
        ranks = dot(both.astype(bf16), chosen[...], NT)
        rank_of = ranks[0:1] * 256.0 + ranks[1:2]
        return iota((1, ROWS), 1) - rank_of.astype(i32), rank_of[:, ROWS - 1 : ROWS].astype(i32)

    everyone = range(GROUPS)

    def repeat(step):
        def once(g, _):
            step(g)
            return 0

        lax.fori_loop(0, GROUPS, once, 0)

    finish(0, 1, early)
    pl.semaphore_wait(barrier, len(partners))
    first(0, 1)
    second(0, 1, 0)
    pick(0)
    pack(0, 0)
    first(0, 0)
    second(0, 0, 0)
    pick(2)
    pack(0, 2)
    first(0, 2)
    second(0, 2, 0)
    meta_first()

    def other_half(i, _):
        part = pl.ds(pl.multiple_of(i * 64, 64), 64)
        e = embed[part, HALF:WIDTH]
        unit[part, HALF:WIDTH] = (e * jnp.tile(scale[part, :], (1, 4))).astype(bf16)
        return 0

    lax.fori_loop(0, 12, other_half, 0)
    pack(1, 1)
    first(1, 1)
    for d in (1, 3, 2):
        for g in everyone:
            second(0, g, d)
    pack(1, 0)
    first(1, 0)
    second(1, 0, 0)
    pack(1, 2)
    first(1, 2)
    second(1, 1, 0)
    second(1, 2, 0)
    meta_second()
    for d in (0, 1, 3, 2):
        for g in (2, 0, 1):
            third(0, g, d)
    meta_third()
    for d in (1, 3, 2):
        for g in everyone:
            second(1, g, d)
    for g in (2, 0, 1):
        third(1, g, 0)
    begin, last_rank = choose()
    for d in (1, 3):
        for g in (2, 0, 1):
            third(1, g, d)
    repeat(lambda g: unpack(0, g))
    for g in (2, 0, 1):
        third(1, g, 2)
    gather()
    unpack(1, 0)
    unpack(1, 1)
    gather_most()
    unpack(1, 2)
    gather_rest()

    here = []
    for j in range(3):
        n = 256 * (j + 1)
        p = slice(256 * j, n)
        s = dot(own[0, 0:n], own[0, p], NT) + dot(own[1, 0:n], own[1, p], NT)
        q, at = iota((n, 256), 0), iota((n, 256), 1) + 256 * j
        s = jnp.where((q >= begin[:, p]) & (q < at), s, -1.0)
        here.append(jnp.max(s, axis=0, keepdims=True))
    best = jnp.concatenate(here, axis=1)

    landed(from_next.at[0], halo_sem.at[1])
    with_next[...] = dot(own[0], from_next[0], NT)
    landed(from_prev.at[0], halo_sem.at[0])
    with_prev[...] = dot(from_prev[0], own[0], NT)

    for h in range(2):
        for g in range(GROUPS):
            for phase in range(2):
                landed(sent0.at[h, g, pl.ds(0, 3)], out_sem.at[h, g, phase])
            landed(unit.at[pl.ds(0, 224)], out_sem.at[h, g, 2])
    landed(meta0.at[pl.ds(0, 3)], mout_sem.at[0])
    landed(meta0.at[pl.ds(0, 3)], mout_sem.at[1])
    landed(flat.at[pl.ds(0, 112)], mout_sem.at[2])

    for i, (lo, hi) in enumerate(PARTS[:2]):
        landed(from_next.at[1, pl.ds(lo, hi - lo)], last_sem.at[i])
        s = with_next[:, lo:hi] + dot(own[1], from_next[1, lo:hi], NT)
        s = jnp.where(iota((ROWS, hi - lo), 0) >= ROWS - 1 - last_rank, s, -1.0)
        answer[:, lo:hi] = jnp.max(s, axis=0, keepdims=True)
    remote(answer, returned, back_out, back_sem, later)

    for i, (lo, hi) in enumerate(PARTS[2:]):
        lo, hi = lo - EDGE, hi - EDGE
        landed(from_prev.at[1, pl.ds(lo, hi - lo)], last_sem.at[2 + i])
        s = with_prev[lo:hi, :] + dot(from_prev[1, lo:hi], own[1], NT)
        s = jnp.where(iota((hi - lo, ROWS), 0) + (lo - REST) >= begin, s, -1.0)
        best = jnp.maximum(best, jnp.max(s, axis=0, keepdims=True))
    landed(from_prev.at[0], halo_out.at[0])
    landed(from_next.at[0], halo_out.at[1])
    for i, (lo, hi) in enumerate(PARTS):
        landed(own.at[1, pl.ds(lo, hi - lo)], last_out.at[i])
    landed(returned, back_sem)
    back = jnp.concatenate([returned[...], jnp.full((1, ROWS - EDGE), -1.0, f32)], axis=1)
    best = jnp.maximum(best, jnp.where(begin < 0, back, -1.0))
    best_ref[...] = best.reshape(ROWS)
    landed(returned, back_out)


def per_device(embed, cluster, rank, target):
    blocks = (2, GROUPS, 4, 4, 4, 2, 16, 128)
    meta = (4, 4, 4, 2, 1, 128)
    dma = pltpu.SemaphoreType.DMA
    best = pl.pallas_call(
        kernel,
        out_shape=pltpu.VMEM((ROWS,), f32),
        in_specs=[
            pl.BlockSpec(memory_space=pl.ANY),
            pl.BlockSpec(memory_space=pl.ANY),
            pl.BlockSpec(memory_space=pl.ANY),
        ],
        out_specs=pl.BlockSpec(memory_space=pltpu.VMEM),
        scratch_shapes=[
            pltpu.VMEM((ROWS,), i32),
            pltpu.VMEM((ROWS,), i32),
            pltpu.VMEM((ROWS, WIDTH), f32),
            pltpu.VMEM((ROWS, 128), f32),
            pltpu.VMEM((GROUPS, DEVICES * DEPTH, ROWS), bf16),
            pltpu.VMEM((ROWS, WIDTH), bf16),
            *[pltpu.VMEM(blocks, bf16)] * 4,
            *[pltpu.VMEM(meta, f32)] * 4,
            pltpu.VMEM((DEVICES, 128), f32),
            pltpu.VMEM((2, GROUPS * 512, HALF), bf16),
            pltpu.VMEM((ROWS, GROUPS * 512), bf16),
            pltpu.VMEM((ROWS, HALF), f32),
            pltpu.VMEM((2, ROWS, HALF), bf16),
            pltpu.VMEM((2, REST, HALF), bf16),
            pltpu.VMEM((2, EDGE, HALF), bf16),
            pltpu.VMEM((REST, ROWS), f32),
            pltpu.VMEM((ROWS, EDGE), f32),
            pltpu.VMEM((1, EDGE), f32),
            pltpu.VMEM((1, EDGE), f32),
            dma((3,)),
            dma((2,)),
            dma((2, GROUPS, 4)),
            dma((2, GROUPS, 4)),
            dma((2, GROUPS)),
            dma((2, GROUPS, 3)),
            dma,
            dma,
            dma,
            dma((3,)),
            dma((2,)),
            dma((2,)),
            dma((4,)),
            dma((4,)),
            dma,
            dma,
        ],
        compiler_params=pltpu.CompilerParams(
            collective_id=0, has_side_effects=True, vmem_limit_bytes=56 * 2**20
        ),
        cost_estimate=pl.CostEstimate(flops=12 * 10**9, bytes_accessed=3 * 2**20, transcendentals=768),
    )(embed, target, rank)
    return best


def solution(mesh):
    in_specs = (P(("grp", "sub"), None), P(("grp", "sub")), P(("grp", "sub")), P(("grp", "sub")))
    out_specs = P(("grp", "sub"))
    return jax.shard_map(
        per_device, mesh=mesh, in_specs=in_specs, out_specs=out_specs, check_vma=False
    )
```
